32 devices in a mesh: lat: 4 (over x, core), lon: 8 (over z, y).
Axes of the slice: x: 2, y: 2, z: 4, core: 2. Of those that a mesh axis runs over, the one named last changes fastest.
Arguments:
- fields: bfloat16 [128, 1024, 128], P('lat', 'lon'), may hold values from -6 to 6
- cotangent: bfloat16 [128, 1024, 128], P('lat', 'lon'), may hold values from -6 to 6
- kernel_bank: bfloat16 [256, 9, 128, 128], P(('lat', 'lon')), may hold values from -0.1875 to 0.1875
- block_expert: int32 [8, 64], P('lat', 'lon'), may hold values from 0 to 255, as said below
- owner: int32 [256], replicated, may hold values from 0 to 255, as said below
Outputs:
- outputs: bfloat16 [128, 1024, 128], P('lat', 'lon')
- grad_fields: bfloat16 [128, 1024, 128], P('lat', 'lon')
- grad_bank: float32 [256, 9, 128, 128], P(('lat', 'lon'))
The draws below stay inside these ranges and needn't reach their ends.
Inputs may be any that keep to these rules, and one draw needn't show every extreme that they name: owner is a permutation: each expert is stored in exactly one row of kernel_bank. `block_expert`: call the lon column of expert e the value (owner[e] // 8) modulo the number of devices along lon. Among the 2 x 8 blocks of one device, at most 2 name experts of any one lon column; in every latitude band of devices one column is named by exactly 2 blocks of each device of that band.
All inputs are finite; a program needn't handle non-finite values.
Results may differ from the reference program's by a relative error of at most 0.0032.
Values may be sent and summed in bfloat16 or wider, within the bound.
No kernel may reach another device: no remote copies, remote signals or barrier semaphores. Data moves between devices by JAX's collectives and lax.ppermute only.
A program may use at most 192 MiB of HBM per device.

```python
import jax
import jax.numpy as jnp
from jax import lax

C = 128
EXPERTS = 256
BS = 16
CAP = 2
BLAT_DEV = 2
BLON_DEV = 8
EXP_DEV = 8
EXP_COL = 32
NBLAT = 8
NBLON = 64
HEIGHT = 128
WIDTH = 1024


def storage_slots(key):
    return jax.random.permutation(jax.random.fold_in(key, 11), EXPERTS).astype(jnp.int32)


def draw_owner(key, part):
    return storage_slots(key)


def draw_block_expert(key, part):
    slots = storage_slots(key)
    holder = jnp.argsort(slots, stable=True).astype(jnp.int32)
    lat_devices = NBLAT // BLAT_DEV
    lon_devices = NBLON // BLON_DEV
    block_total = BLAT_DEV * BLON_DEV
    entry_total = lon_devices * CAP
    full_column = jax.random.randint(jax.random.fold_in(key, 23), (lat_devices,), 0, lon_devices)

    def one_device(device_index):
        device_key = jax.random.fold_in(jax.random.fold_in(key, 37), device_index)
        band = device_index // lon_devices
        entries = jax.random.permutation(jax.random.fold_in(device_key, 1), entry_total).astype(jnp.int32)
        columns = entries // CAP
        ranking = jnp.where(columns == full_column[band], -1, jnp.arange(entry_total, dtype=jnp.int32))
        ordered = entries[jnp.argsort(ranking, stable=True)]
        picked = ordered[:block_total] // CAP
        mixing = jax.random.permutation(jax.random.fold_in(device_key, 2), block_total)
        placed = picked[mixing]
        first_pick = jax.random.randint(jax.random.fold_in(device_key, 3), (block_total,), 0, EXP_COL)
        second_pick = jax.random.randint(jax.random.fold_in(device_key, 4), (block_total,), 0, EXP_COL)
        local_ids = jnp.minimum(first_pick, second_pick)
        stored = (local_ids // EXP_DEV * lon_devices + placed) * EXP_DEV + local_ids % EXP_DEV
        return holder[stored]
    table = jax.vmap(one_device)(jnp.arange(lat_devices * lon_devices, dtype=jnp.int32))
    table = table.reshape(lat_devices, lon_devices, BLAT_DEV, BLON_DEV).transpose(0, 2, 1, 3)
    return table.reshape(NBLAT, NBLON).astype(jnp.int32)


def steps_of(own_key, extent, split, least, high):
    level = 1.0
    for dim, shards_of in split:
        heights = jax.random.uniform(jax.random.fold_in(jax.random.fold_in(own_key, 6), dim), (shards_of,), jnp.float32, least / len(split), high / len(split))
        level = level * jnp.repeat(jnp.exp(heights), extent[dim] // shards_of).reshape((-1,) + (1,) * (len(extent) - 1 - dim))
    return level


def scatter_about(rng, extent, scale, most, cuts=(), kind=jnp.bfloat16):
    level = steps_of(rng, extent, cuts, -0.22, 0.18) if cuts else 1.0
    array = jax.random.normal(rng, extent, jnp.float32) * scale * level
    return jnp.minimum(jnp.maximum(array, -most), most).astype(kind)


def setup_inputs(seed: int = 0) -> dict:
    arg_keys = jax.random.split(jax.random.key(seed), 6)
    return {
        "fields": scatter_about(arg_keys[0], (HEIGHT, WIDTH, C), 1.0, 6.0, ((0, 4), (1, 8))),
        "cotangent": scatter_about(arg_keys[1], (HEIGHT, WIDTH, C), 1.0, 6.0, ((0, 4), (1, 8))),
        "kernel_bank": scatter_about(arg_keys[2], (EXPERTS, 9, C, C), (9 * C) ** -0.5, 0.1875, ((0, 32),)),
        "block_expert": draw_block_expert(jax.random.fold_in(arg_keys[5], 71), 0),
        "owner": draw_owner(jax.random.fold_in(arg_keys[5], 71), 0),
    }


def windows(source, along):
    blocks_n = (source.shape[along] - 2) // BS
    leading = lax.slice_in_dim(source, 0, BS * blocks_n, axis=along)
    trailing = lax.slice_in_dim(source, BS, BS * blocks_n + 2, axis=along)
    padding = [(0, 0)] * source.ndim
    padding[along] = (0, BS - 2)
    trailing = jnp.pad(trailing, padding)
    new_shape = source.shape[:along] + (blocks_n, BS) + source.shape[along + 1:]
    leading = leading.reshape(new_shape)
    trailing = lax.slice_in_dim(trailing.reshape(new_shape), 0, 2, axis=along + 1)
    return jnp.concatenate([leading, trailing], axis=along + 1)


def tiles_to_grid(blocks):
    lat_blocks, lon_blocks, tile_rows, tile_cols, chans = blocks.shape
    return blocks.transpose(0, 2, 1, 3, 4).reshape(lat_blocks * tile_rows, lon_blocks * tile_cols, chans)


def place_portion(portion, row_shift, col_shift):
    padded = jnp.pad(portion, ((0, 0), (0, 0), (0, BS - portion.shape[2]), (0, BS - portion.shape[3]), (0, 0)))
    grid = tiles_to_grid(padded)
    return jnp.pad(grid, ((row_shift, BS - row_shift), (col_shift, BS - col_shift), (0, 0)))


def place_blocks(blocks):
    row_total = blocks.shape[0] * BS
    col_total = blocks.shape[1] * BS
    canvas = place_portion(blocks[:, :, :BS, :BS], 0, 0)
    canvas = canvas + place_portion(blocks[:, :, :BS, BS:], 0, BS)
    canvas = canvas + place_portion(blocks[:, :, BS:, :BS], BS, 0)
    canvas = canvas + place_portion(blocks[:, :, BS:, BS:], BS, BS)
    return canvas[:row_total + 2, :col_total + 2]


def block_math(patch_in, cot_in, kernel_in):
    patch_f = patch_in.astype(jnp.float32)
    cot_f = cot_in.astype(jnp.float32)
    kernel_f = kernel_in.astype(jnp.float32)
    hp = lax.Precision.HIGHEST
    total = jnp.zeros(cot_in.shape, jnp.float32)
    spread = jnp.zeros(patch_in.shape, jnp.float32)
    grads = []
    for tap_index in range(9):
        row_off = tap_index // 3
        col_off = tap_index % 3
        window = patch_f[:, row_off:row_off + BS, col_off:col_off + BS]
        total = total + jnp.einsum("sxyc,scd->sxyd", window, kernel_f[:, tap_index], precision=hp)
        term = jnp.einsum("sxyd,scd->sxyc", cot_f, kernel_f[:, tap_index], precision=hp)
        spread = spread + jnp.pad(term, ((0, 0), (row_off, 2 - row_off), (col_off, 2 - col_off), (0, 0)))
        grads.append(jnp.einsum("sxyc,sxyd->scd", window, cot_f, precision=hp))
    return total, spread, jnp.stack(grads, axis=1)


def reference(fields, cotangent, kernel_bank, block_expert, owner):
    height, width, chans = fields.shape
    wrapped = jnp.concatenate([fields[:, -1:], fields, fields[:, :1]], axis=1)
    extended = jnp.pad(wrapped, ((1, 1), (0, 0), (0, 0)))
    patches = windows(windows(extended, 0), 2).transpose(0, 2, 1, 3, 4)
    cot_blocks = cotangent.reshape(NBLAT, BS, NBLON, BS, chans).transpose(0, 2, 1, 3, 4)
    storage = owner[block_expert].astype(jnp.int32)

    def one_row(grad_carry, inputs):
        row_patches, row_cot, row_storage = inputs
        kernels = kernel_bank[row_storage]
        total, spread, per_block = block_math(row_patches, row_cot, kernels)
        grad_carry = grad_carry.at[row_storage].add(per_block)
        return grad_carry, (total.astype(jnp.bfloat16), spread.astype(jnp.bfloat16))

    start_grad = jnp.zeros((EXPERTS, 9, chans, chans), jnp.float32)
    grad_bank, (out_blocks, spread_blocks) = lax.scan(one_row, start_grad, (patches, cot_blocks, storage))
    outputs = tiles_to_grid(out_blocks)
    canvas = place_blocks(spread_blocks.astype(jnp.float32))
    middle = canvas[1:height + 1]
    result = middle[:, 1:width + 1]
    result = result.at[:, 0].add(middle[:, width + 1])
    result = result.at[:, width - 1].add(middle[:, 0])
    return outputs, result.astype(jnp.bfloat16), grad_bank
```

```python
import functools

import jax
import jax.numpy as jnp
from jax import lax
from jax.experimental import pallas as pl
from jax.experimental.pallas import tpu as pltpu
from jax.sharding import PartitionSpec as P

BS = 16
CAP = 2
EDGE = BS + 2
CELLS = BS * BS
MAIN = EDGE * BS
TAIL = 48
ROWS = CELLS + MAIN + TAIL
SIDE = CELLS + MAIN
NUMBER = 2 * EDGE
GAP = 8
SPAN = 2 * BS
F32 = jnp.float32
BF16 = jnp.bfloat16


def params(mib):
    return pltpu.CompilerParams(vmem_limit_bytes=mib * 1024 * 1024)


def whole(memory=pltpu.VMEM):
    return pl.BlockSpec(memory_space=memory)


def plan_slots(experts, owner, blocks, numbers, counts, per, columns):
    lat_blocks, lon_blocks = experts.shape

    def clear_slot(s, carry):
        blocks[s] = -1
        numbers[s] = 0
        return carry

    def clear_count(s, carry):
        counts[s] = 0
        return carry

    lax.fori_loop(0, columns * CAP, clear_slot, 0)
    lax.fori_loop(0, columns, clear_count, 0)

    def place(b, carry):
        stored = owner[experts[lax.div(b, lon_blocks), lax.rem(b, lon_blocks)]]
        group = lax.div(stored, per)
        column = lax.rem(group, columns)
        rank = counts[column]
        counts[column] = rank + 1
        slot = column * CAP + rank
        blocks[slot] = b
        numbers[slot] = lax.div(group, columns) * per + lax.rem(stored, per)
        return carry

    lax.fori_loop(0, lat_blocks * lon_blocks, place, 0)


def dispatch_kernel(
    per, columns, experts, owner, fields, cot, north, south, west, east, out,
    rows, wide, tail, blocks, numbers, counts,
):
    height, width = fields.shape[:2]
    lon_blocks = width // BS
    stride = width + 2 * GAP
    step = pl.program_id(0)

    @pl.when(step == 0)
    def _():
        plan_slots(experts, owner, blocks, numbers, counts, per, columns)
        rows[0] = north[0]
        rows[height + 1] = south[0]

        def fill(r, carry):
            rows[r + 1] = fields[r]
            return carry

        lax.fori_loop(0, height, fill, 0)

        def widen(r, carry):
            start = pl.multiple_of(r * stride + GAP, 8)
            wide[pl.ds(start, width), :] = rows[r].astype(F32)
            return carry

        lax.fori_loop(0, height + 2, widen, 0)
        wide[pl.ds(GAP - 1, height + 2, stride=stride), :] = west[...].astype(F32)
        wide[pl.ds(GAP + width, height + 2, stride=stride), :] = east[...].astype(F32)

    for r in range(CAP):
        slot = step * CAP + r
        held = blocks[slot]
        block = jnp.maximum(held, 0)
        top = lax.div(block, lon_blocks) * BS
        left = pl.multiple_of(lax.rem(block, lon_blocks) * BS, BS)

        @pl.when(held >= 0)
        def _():
            part = cot[pl.ds(top, BS), pl.ds(left, BS), :]
            out[0, r, 0:CELLS, :] = part.reshape(CELLS, part.shape[2])

        @pl.when(held < 0)
        def _():
            out[0, r, 0:CELLS, :] = jnp.zeros((CELLS, out.shape[3]), BF16)

        window = rows[pl.ds(top, EDGE), pl.ds(left, BS), :]
        out[0, r, CELLS:SIDE, :] = window.reshape(MAIN, window.shape[2])
        start = top * stride + left
        tail[0:EDGE, :] = wide[pl.ds(start + GAP - 1, EDGE, stride=stride), :]
        tail[EDGE : 2 * EDGE, :] = wide[pl.ds(start + GAP + BS, EDGE, stride=stride), :]
        tail[NUMBER:TAIL, :] = jnp.full(
            (TAIL - NUMBER, tail.shape[1]), numbers[slot].astype(F32), F32
        )
        out[0, r, SIDE:ROWS, :] = tail[...].astype(BF16)


def dispatch(experts, owner, fields, cot, north, south, west, east, per, columns):
    height, width, chans = fields.shape
    return pl.pallas_call(
        functools.partial(dispatch_kernel, per, columns),
        grid=(columns,),
        out_shape=jax.ShapeDtypeStruct((columns, CAP, ROWS, chans), BF16),
        in_specs=[whole(pltpu.SMEM)] * 2 + [whole()] * 6,
        out_specs=pl.BlockSpec((1, CAP, ROWS, chans), lambda q: (q, 0, 0, 0)),
        scratch_shapes=[
            pltpu.VMEM((height + 2, width, chans), BF16),
            pltpu.VMEM(((height + 2) * (width + 2 * GAP), chans), F32),
            pltpu.VMEM((TAIL, chans), F32),
            pltpu.SMEM((columns * CAP,), jnp.int32),
            pltpu.SMEM((columns * CAP,), jnp.int32),
            pltpu.SMEM((columns,), jnp.int32),
        ],
        compiler_params=params(32),
        cost_estimate=pl.CostEstimate(flops=0, bytes_accessed=6_000_000, transcendentals=0),
        name="dispatch",
    )(experts, owner, fields, cot, north, south, west, east)


def window_rows(slot, tail):
    chans = tail.shape[1]
    tail[...] = slot[SIDE:ROWS, :].astype(F32)
    parts = []
    for a in range(3):
        start = CELLS + a * BS
        sides = jnp.concatenate(
            [tail[a : a + BS, :], tail[EDGE + a : EDGE + a + BS, :]], axis=0
        ).astype(BF16)
        parts.append(jnp.concatenate([slot[start : start + CELLS, :], sides], axis=0))
    return jnp.concatenate(parts, axis=1)


def taps_kernel(per, *refs):
    place, slot = refs[:2]
    banks = refs[2:-6]
    out, held, tail, early, late, sems = refs[-6:]
    chans = out.shape[3]
    step = pl.program_id(0)
    total = pl.num_programs(0)

    def fetch(s, buffer):
        index = place[s]
        piece = lax.div(index, per)
        row = lax.rem(index, per)
        for p, bank in enumerate(banks):

            @pl.when(piece == p)
            def _():
                pltpu.make_async_copy(bank.at[row], held.at[buffer], sems.at[buffer]).start()

    now = lax.rem(step, 2)

    @pl.when(step == 0)
    def _():
        early[...] = jnp.zeros(early.shape, F32)
        late[...] = jnp.zeros(late.shape, F32)
        fetch(step, now)

    @pl.when(step + 1 < total)
    def _():
        fetch(step + 1, 1 - now)

    pltpu.make_async_copy(banks[0].at[0], held.at[now], sems.at[now]).wait()
    data = slot.at[0, 0]
    kernel = [held[now, t] for t in range(9)]

    cot = data[0:CELLS, :]
    shifted = []
    for a in range(3):
        pieces = []
        if a > 0:
            pieces.append(jnp.zeros((a * BS, chans), BF16))
        pieces.append(cot)
        if a < 2:
            pieces.append(jnp.zeros(((2 - a) * BS, chans), BF16))
        shifted.append(jnp.concatenate(pieces, axis=0))
    spread_rows = jnp.concatenate(shifted, axis=1)
    spread_mat = jnp.concatenate(
        [jnp.concatenate([kernel[3 * a + b] for a in range(3)], axis=1) for b in range(3)], axis=0
    )
    spread = lax.dot_general(
        spread_rows, spread_mat, (((1,), (1,)), ((), ())), preferred_element_type=F32
    )
    for u in range(EDGE):
        early[SPAN * u + 8 : SPAN * u + 8 + BS, :] = spread[BS * u : BS * u + BS, 0:chans]
        late[SPAN * u + 8 : SPAN * u + 8 + BS, :] = spread[BS * u : BS * u + BS, 2 * chans :]
    tail[0:EDGE, :] = early[pl.ds(8, EDGE, stride=SPAN), :]
    tail[EDGE : 2 * EDGE, :] = late[pl.ds(8 + BS - 1, EDGE, stride=SPAN), :]
    tail[NUMBER:TAIL, :] = jnp.zeros((TAIL - NUMBER, chans), F32)
    out[0, 0, SIDE:ROWS, :] = tail[...].astype(BF16)
    zero = jnp.zeros((EDGE, chans), F32)
    early[pl.ds(8 + BS, EDGE, stride=SPAN), :] = zero
    late[pl.ds(7, EDGE, stride=SPAN), :] = zero
    for u in range(EDGE):
        line = (
            spread[BS * u : BS * u + BS, chans : 2 * chans]
            + early[SPAN * u + 9 : SPAN * u + 9 + BS, :]
            + late[SPAN * u + 7 : SPAN * u + 7 + BS, :]
        )
        out[0, 0, CELLS + BS * u : CELLS + BS * u + BS, :] = line.astype(BF16)

    rows = window_rows(data, tail)
    forward_mat = jnp.concatenate(
        [jnp.concatenate([kernel[3 * a + b] for b in range(3)], axis=1) for a in range(3)], axis=0
    )
    result = jnp.dot(rows, forward_mat, preferred_element_type=F32)
    for x in range(BS):
        early[SPAN * x + 8 : SPAN * x + 8 + BS, :] = result[BS * x : BS * x + BS, 0:chans]
        late[SPAN * x + 8 : SPAN * x + 8 + BS, :] = result[BS * x : BS * x + BS, 2 * chans :]
    early[pl.ds(7, BS, stride=SPAN), :] = result[CELLS : CELLS + BS, 0:chans]
    late[pl.ds(8 + BS, BS, stride=SPAN), :] = result[CELLS + BS :, 2 * chans :]
    for x in range(BS):
        line = (
            result[BS * x : BS * x + BS, chans : 2 * chans]
            + early[SPAN * x + 7 : SPAN * x + 7 + BS, :]
            + late[SPAN * x + 9 : SPAN * x + 9 + BS, :]
        )
        out[0, 0, BS * x : BS * x + BS, :] = line.astype(BF16)


def taps(place, slots, banks):
    columns, cap, rows, chans = slots.shape
    per = banks[0].shape[0]
    spec = pl.BlockSpec((1, 1, rows, chans), lambda s: (s // cap, s % cap, 0, 0))
    return pl.pallas_call(
        functools.partial(taps_kernel, per),
        grid=(columns * cap,),
        out_shape=jax.ShapeDtypeStruct(slots.shape, BF16),
        in_specs=[whole(pltpu.SMEM), spec] + [whole(pl.ANY)] * len(banks),
        out_specs=spec,
        scratch_shapes=[
            pltpu.VMEM((2,) + banks[0].shape[1:], BF16),
            pltpu.VMEM((TAIL, chans), F32),
            pltpu.VMEM((EDGE * SPAN, chans), F32),
            pltpu.VMEM((EDGE * SPAN, chans), F32),
            pltpu.SemaphoreType.DMA((2,)),
        ],
        compiler_params=params(32),
        cost_estimate=pl.CostEstimate(
            flops=2_800_000_000, bytes_accessed=10_000_000, transcendentals=0
        ),
        name="taps",
    )(place, slots, *banks)


def grads_kernel(first, terms, place, slots, *refs):
    added = refs[:terms]
    out, total, tail, cells = refs[terms:]
    columns, cap, _, chans = slots.shape
    wanted = first + pl.program_id(0)
    if terms:
        start = added[0][0].astype(F32)
        for term in added[1:]:
            start = start + term[0].astype(F32)
        total[...] = start
    else:
        total[...] = jnp.zeros(total.shape, F32)

    def visit(s, carry):
        @pl.when(place[s] == wanted)
        def _():
            data = slots.at[lax.div(s, cap), lax.rem(s, cap)]
            cot = data[0:CELLS, :]
            cells[8 : 8 + CELLS, :] = cot.astype(F32)
            column = lax.rem(lax.broadcasted_iota(jnp.int32, (CELLS, chans), 0), BS)
            after = jnp.where(column == BS - 1, 0.0, cells[9 : 9 + CELLS, :]).astype(BF16)
            before = jnp.where(column == 0, 0.0, cells[7 : 7 + CELLS, :]).astype(BF16)
            initial = cells[pl.ds(8, BS, stride=BS), :].astype(BF16)
            last = cells[pl.ds(8 + BS - 1, BS, stride=BS), :].astype(BF16)
            zero = jnp.zeros((BS, chans), BF16)
            right = jnp.concatenate(
                [
                    jnp.concatenate([after, initial, zero], axis=0),
                    jnp.concatenate([cot, zero, zero], axis=0),
                    jnp.concatenate([before, zero, last], axis=0),
                ],
                axis=1,
            )
            rows = window_rows(data, tail)
            term = lax.dot_general(
                rows, right, (((0,), (0,)), ((), ())), preferred_element_type=F32
            )
            for a in range(3):
                for b in range(3):
                    total[3 * a + b] += term[
                        a * chans : (a + 1) * chans, b * chans : (b + 1) * chans
                    ]

        return carry

    lax.fori_loop(0, columns * cap, visit, 0)
    out[0] = total[...].astype(out.dtype)


def grads(place, slots, piece, bank_shape, added, dtype):
    per, taps_n, chans, outs = bank_shape
    spec = pl.BlockSpec((1, taps_n, chans, outs), lambda e: (e, 0, 0, 0))
    return pl.pallas_call(
        functools.partial(grads_kernel, piece * per, len(added)),
        grid=(per,),
        out_shape=jax.ShapeDtypeStruct(bank_shape, dtype),
        in_specs=[whole(pltpu.SMEM), whole()] + [spec] * len(added),
        out_specs=spec,
        scratch_shapes=[
            pltpu.VMEM((taps_n, chans, outs), F32),
            pltpu.VMEM((TAIL, chans), F32),
            pltpu.VMEM((CELLS + 16, chans), F32),
        ],
        compiler_params=params(32),
        cost_estimate=pl.CostEstimate(
            flops=500_000_000, bytes_accessed=6_000_000, transcendentals=0
        ),
        name="grads",
    )(place, slots, *added)


def collect_kernel(
    per, columns, experts, owner, slots, outputs, canvas, north, south, west, east,
    tail, blocks, numbers, counts,
):
    height, width, chans = outputs.shape
    lon_blocks = width // BS
    stride = width + 2 * GAP
    plan_slots(experts, owner, blocks, numbers, counts, per, columns)

    def clear(r, carry):
        start = pl.multiple_of(r * stride, 8)
        canvas[pl.ds(start, stride), :] = jnp.zeros((stride, chans), F32)
        return carry

    lax.fori_loop(0, height + 2, clear, 0)

    def visit(s, carry):
        held = blocks[s]

        @pl.when(held >= 0)
        def _():
            data = slots.at[lax.div(s, CAP), lax.rem(s, CAP)]
            top = lax.div(held, lon_blocks) * BS
            left = pl.multiple_of(lax.rem(held, lon_blocks) * BS, BS)
            outputs[pl.ds(top, BS), pl.ds(left, BS), :] = data[0:CELLS, :].reshape(BS, BS, chans)
            for u in range(EDGE):
                place = pl.ds(pl.multiple_of((top + u) * stride + GAP + left, 8), BS)
                line = data[CELLS + BS * u : CELLS + BS * u + BS, :].astype(F32)
                canvas[place, :] = canvas[place, :] + line
            tail[...] = data[SIDE:ROWS, :].astype(F32)
            start = top * stride + left
            place = pl.ds(start + GAP - 1, EDGE, stride=stride)
            canvas[place, :] = canvas[place, :] + tail[0:EDGE, :]
            place = pl.ds(start + GAP + BS, EDGE, stride=stride)
            canvas[place, :] = canvas[place, :] + tail[EDGE : 2 * EDGE, :]

        return carry

    lax.fori_loop(0, columns * CAP, visit, 0)
    north[...] = canvas[0:stride, :].astype(BF16)
    south[...] = canvas[(height + 1) * stride : (height + 2) * stride, :].astype(BF16)
    west[...] = canvas[pl.ds(stride + GAP - 1, height, stride=stride), :]
    east[...] = canvas[pl.ds(stride + GAP + width, height, stride=stride), :]


def collect(experts, owner, slots, shape, per):
    height, width, chans = shape
    columns = slots.shape[0]
    stride = width + 2 * GAP
    return pl.pallas_call(
        functools.partial(collect_kernel, per, columns),
        out_shape=(
            jax.ShapeDtypeStruct(shape, BF16),
            jax.ShapeDtypeStruct(((height + 2) * stride, chans), F32),
            jax.ShapeDtypeStruct((stride, chans), BF16),
            jax.ShapeDtypeStruct((stride, chans), BF16),
            jax.ShapeDtypeStruct((height, chans), F32),
            jax.ShapeDtypeStruct((height, chans), F32),
        ),
        in_specs=[whole(pltpu.SMEM)] * 2 + [whole()],
        out_specs=(whole(),) * 6,
        scratch_shapes=[
            pltpu.VMEM((TAIL, chans), F32),
            pltpu.SMEM((columns * CAP,), jnp.int32),
            pltpu.SMEM((columns * CAP,), jnp.int32),
            pltpu.SMEM((columns,), jnp.int32),
        ],
        compiler_params=params(32),
        cost_estimate=pl.CostEstimate(flops=0, bytes_accessed=8_000_000, transcendentals=0),
        name="collect",
    )(experts, owner, slots)


def finish_kernel(canvas, north, south, west, east, out):
    height, width, chans = out.shape
    stride = width + 2 * GAP
    column = lax.broadcasted_iota(jnp.int32, (BS, chans), 0)
    for r in range(height):
        start = (r + 1) * stride + GAP
        line = canvas[start : start + width, :]
        if r == 0:
            line = line + north[GAP : GAP + width, :].astype(F32)
        if r == height - 1:
            line = line + south[GAP : GAP + width, :].astype(F32)
        first = line[:BS] + jnp.where(column == 0, west[r : r + 1, :].astype(F32), 0.0)
        last = line[width - BS :] + jnp.where(
            column == BS - 1, east[r : r + 1, :].astype(F32), 0.0
        )
        out[r] = jnp.concatenate([first, line[BS : width - BS], last], axis=0).astype(BF16)


def finish(canvas, north, south, west, east, shape):
    return pl.pallas_call(
        finish_kernel,
        out_shape=jax.ShapeDtypeStruct(shape, BF16),
        in_specs=[whole()] * 5,
        out_specs=whole(),
        compiler_params=params(32),
        cost_estimate=pl.CostEstimate(flops=0, bytes_accessed=4_000_000, transcendentals=0),
        name="finish",
    )(canvas, north, south, west, east)


def across(array, axis, shift, wrap):
    count = lax.axis_size(axis)
    pairs = [(i, i + shift) for i in range(count)]
    if wrap:
        pairs = [(i, j % count) for i, j in pairs]
    else:
        pairs = [(i, j) for i, j in pairs if 0 <= j < count]
    return lax.ppermute(array, axis, pairs)


def to_other_core(array):
    return lax.ppermute(array, "lat", [(i, i ^ 1) for i in range(lax.axis_size("lat"))])


def to_chip(array, shift):
    count = lax.axis_size("lat")
    return lax.ppermute(array, "lat", [(i, (i + 2 * shift) % count) for i in range(count)])


def swap(slots):
    return lax.all_to_all(slots, "lon", split_axis=0, concat_axis=0, tiled=True)


def local(fields, cotangent, kernel_bank, block_expert, owner):
    columns = lax.axis_size("lon")
    lat_count = lax.axis_size("lat")
    chips = lat_count // 2
    lat_index = lax.axis_index("lat")
    height, width, chans = fields.shape
    per = kernel_bank.shape[0]

    north = across(fields[height - 1 :], "lat", 1, False)
    south = across(fields[:1], "lat", -1, False)
    first = jnp.concatenate([north[:, 0], fields[:, 0], south[:, 0]], axis=0)
    last = jnp.concatenate([north[:, -1], fields[:, -1], south[:, -1]], axis=0)
    west = across(last, "lon", 1, True)
    east = across(first, "lon", -1, True)

    banks = [kernel_bank, to_other_core(kernel_bank)]
    for k in range(1, chips):
        far = to_chip(kernel_bank, -k)
        banks += [far, to_other_core(far)]

    sent = dispatch(
        block_expert, owner, fields, cotangent, north, south, west, east, per, columns
    )
    slots = swap(sent)
    numbers = slots[:, :, SIDE + NUMBER, 0].reshape(-1).astype(jnp.int32)
    owner_lat = numbers // per
    chip_step = (owner_lat // 2 - lat_index // 2 + chips) % chips
    core_step = (owner_lat % 2 - lat_index % 2 + 2) % 2
    place = (2 * chip_step + core_step) * per + numbers % per

    returned = swap(taps(place, slots, banks))

    shape = kernel_bank.shape
    arrived = []
    for k in range(1, chips):
        part = to_other_core(grads(place, slots, 2 * k + 1, shape, [], BF16))
        arrived.append(to_chip(grads(place, slots, 2 * k, shape, [part], BF16), k))
    arrived.append(to_other_core(grads(place, slots, 1, shape, [], BF16)))
    grad_bank = grads(place, slots, 0, shape, arrived, F32)

    outputs, canvas, top, bottom, left, right = collect(
        block_expert, owner, returned, fields.shape, per
    )
    above = across(bottom, "lat", 1, False)
    below = across(top, "lat", -1, False)

    def with_corners(line, column):
        line = line.at[0].add(above[column].astype(F32))
        return line.at[height - 1].add(below[column].astype(F32)).astype(BF16)

    from_west = across(with_corners(right, GAP + width), "lon", 1, True)
    from_east = across(with_corners(left, GAP - 1), "lon", -1, True)
    grad_fields = finish(canvas, above, below, from_west, from_east, fields.shape)
    return (outputs, grad_fields, grad_bank)


def solution(mesh):
    return jax.shard_map(
        local,
        mesh=mesh,
        in_specs=(
            P("lat", "lon", None),
            P("lat", "lon", None),
            P(("lat", "lon"), None, None, None),
            P("lat", "lon"),
            P(),
        ),
        out_specs=(
            P("lat", "lon", None),
            P("lat", "lon", None),
            P(("lat", "lon"), None, None, None),
        ),
        check_vma=False,
    )
```

```python
import functools

import jax
import jax.numpy as jnp
from jax import lax
from jax.experimental import pallas as pl
from jax.experimental.pallas import tpu as pltpu
from jax.sharding import PartitionSpec as P

BS = 16
CAP = 2
EDGE = BS + 2
CELLS = BS * BS
MAIN = EDGE * BS
TAIL = 48
OWN = 2 * BS
RING = 5
LINES = OWN + RING
NUMBER = 4 * BS + 4
WINDOW = EDGE + TAIL // BS
BACK = BS + WINDOW
GAP = 8
SPAN = 2 * BS
F32 = jnp.float32
BF16 = jnp.bfloat16


def params(mib):
    return pltpu.CompilerParams(vmem_limit_bytes=mib * 1024 * 1024)


TOKEN = jax.ShapeDtypeStruct((8, 128), jnp.float32)


def whole(memory=pltpu.VMEM):
    return pl.BlockSpec(memory_space=memory)


def copy(source, target, sem):
    return pltpu.make_async_copy(source, target, sem)


def corner(block, lon_blocks):
    top = lax.div(block, lon_blocks) * BS
    return top, pl.multiple_of(lax.rem(block, lon_blocks) * BS, BS)


def tables(columns):
    return [
        pltpu.SMEM((columns * CAP,), jnp.int32),
        pltpu.SMEM((columns * CAP,), jnp.int32),
        pltpu.SMEM((columns,), jnp.int32),
    ]


def plan_slots(experts, owner, blocks, numbers, counts, per, columns):
    lat_blocks, lon_blocks = experts.shape

    def clear_slot(s, carry):
        blocks[s] = -1
        numbers[s] = 0
        return carry

    def clear_count(s, carry):
        counts[s] = 0
        return carry

    lax.fori_loop(0, columns * CAP, clear_slot, 0)
    lax.fori_loop(0, columns, clear_count, 0)

    def place(b, carry):
        stored = owner[experts[lax.div(b, lon_blocks), lax.rem(b, lon_blocks)]]
        group = lax.div(stored, per)
        column = lax.rem(group, columns)
        rank = counts[column]
        counts[column] = rank + 1
        slot = column * CAP + rank
        blocks[slot] = b
        numbers[slot] = lax.div(group, columns) * per + lax.rem(stored, per)
        return carry

    lax.fori_loop(0, lat_blocks * lon_blocks, place, 0)


def own_kernel(per, columns, experts, owner, fields, cot, *refs):
    out, grid, cells, blank, blocks, numbers, counts, load_sems, sems = refs
    height, width, chans = fields.shape
    sources = (cells, grid)
    loads = [copy(cot, cells, load_sems.at[0]), copy(fields, grid, load_sems.at[1])]
    for load in loads:
        load.start()
    plan_slots(experts, owner, blocks, numbers, counts, per, columns)
    blank[...] = jnp.zeros(blank.shape, BF16)
    for part, source in enumerate(sources):
        loads[part].wait()
        for column in range(columns):
            for r in range(CAP):
                s = column * CAP + r
                held = blocks[s]
                top, left = corner(jnp.maximum(held, 0), experts.shape[1])
                target = out.at[column, r, pl.ds(part * BS, BS)]

                @pl.when(held >= 0)
                def _():
                    copy(
                        source.at[pl.ds(top, BS), pl.ds(left, BS), :], target, sems.at[part, s]
                    ).start()

                @pl.when(held < 0)
                def _():
                    copy(blank, target, sems.at[part, s]).start()

    for part in range(2):
        for s in range(columns * CAP):
            copy(blank, out.at[0, 0, pl.ds(0, BS)], sems.at[part, s]).wait()


def dispatch_own(experts, owner, fields, cot, per, columns):
    chans = cot.shape[2]
    out = pl.pallas_call(
        functools.partial(own_kernel, per, columns),
        out_shape=[
            jax.ShapeDtypeStruct((columns, CAP, OWN, BS, chans), BF16),
        ],
        in_specs=[whole(pltpu.SMEM)] * 2 + [whole(pltpu.HBM)] * 2,
        out_specs=[whole(pltpu.HBM)],
        scratch_shapes=[
            pltpu.VMEM(fields.shape, BF16),
            pltpu.VMEM(cot.shape, BF16),
            pltpu.VMEM((BS, BS, chans), BF16),
        ]
        + tables(columns)
        + [pltpu.SemaphoreType.DMA((2,)), pltpu.SemaphoreType.DMA((2, columns * CAP))],
        compiler_params=params(60),
        cost_estimate=pl.CostEstimate(flops=0, bytes_accessed=6_000_000, transcendentals=0),
        name="dispatch_own",
    )(experts, owner, fields, cot)
    return out[0]


def rims_kernel(north, south, first, last, first_out, last_out):
    width = north.shape[1]
    for inner, out, left, column in (
        (first, first_out, 0, 0),
        (last, last_out, width - BS, BS - 1),
    ):
        above = north[0, left : left + BS, :].astype(F32)
        below = south[0, left : left + BS, :].astype(F32)
        out[...] = jnp.concatenate(
            [above[column : column + 1], inner[...], below[column : column + 1]], axis=0
        ).astype(BF16)


def rims_of(north, south, first, last):
    height, chans = first.shape
    return pl.pallas_call(
        rims_kernel,
        out_shape=[jax.ShapeDtypeStruct((height + 2, chans), BF16)] * 2,
        in_specs=[whole()] * 4,
        out_specs=[whole()] * 2,
        compiler_params=params(4),
        name="rims",
    )(north, south, first, last)


def corners_kernel(above, below, left, right, _, left_out, right_out):
    height = left.shape[0]
    row = lax.broadcasted_iota(jnp.int32, left.shape, 0)
    stride = above.shape[0]
    for line, out, start, column in (
        (left, left_out, 0, GAP - 1),
        (right, right_out, stride - BS, BS - GAP),
    ):
        top = above[start : start + BS, :].astype(F32)[column : column + 1]
        bottom = below[start : start + BS, :].astype(F32)[column : column + 1]
        out[...] = (
            line[...]
            + jnp.where(row == 0, top, 0.0)
            + jnp.where(row == height - 1, bottom, 0.0)
        ).astype(BF16)


def corners_of(above, below, left, right, after):
    return pl.pallas_call(
        corners_kernel,
        out_shape=[jax.ShapeDtypeStruct(left.shape, BF16)] * 2,
        in_specs=[whole()] * 4 + [whole(pltpu.HBM)],
        out_specs=[whole()] * 2,
        compiler_params=params(4),
        name="corners",
    )(above, below, left, right, after)


def ring_kernel(
    per, columns, me, experts, owner, fields, north, south, west, east, *refs
):
    outs = refs[:columns]
    rows, wide, rings, blocks, numbers, counts, load_sem, sems = refs[columns:]
    height, width, chans = fields.shape
    stride = width + 2 * GAP
    load = copy(fields, rows.at[pl.ds(1, height)], load_sem)
    load.start()
    plan_slots(experts, owner, blocks, numbers, counts, per, columns)
    rows[0] = north[0]
    rows[height + 1] = south[0]
    load.wait()

    def widen(r, carry):
        start = pl.multiple_of(r * stride + GAP, 8)
        wide[pl.ds(start, width), :] = rows[r].astype(F32)
        return carry

    lax.fori_loop(0, height + 2, widen, 0)
    wide[pl.ds(GAP - 1, height + 2, stride=stride), :] = west[...].astype(F32)
    wide[pl.ds(GAP + width, height + 2, stride=stride), :] = east[...].astype(F32)
    for k in range(columns):
        for r in range(CAP):
            s = k * CAP + r
            slot = (me[0] ^ k) * CAP + r
            top, left = corner(jnp.maximum(blocks[slot], 0), experts.shape[1])
            start = pl.multiple_of(top * stride + left, 8)
            upper = wide[pl.ds(start, BS + 2 * GAP), :]
            start = pl.multiple_of(start + (EDGE - 1) * stride, 8)
            lower = wide[pl.ds(start, BS + 2 * GAP), :]
            start = (top + 1) * stride + left
            ring = jnp.concatenate(
                [
                    upper[GAP - 1 : GAP + BS + 1],
                    lower[GAP - 1 : GAP + BS + 1],
                    wide[pl.ds(start + GAP - 1, BS, stride=stride), :],
                    wide[pl.ds(start + GAP + BS, BS, stride=stride), :],
                    jnp.full((RING * BS - NUMBER, chans), numbers[slot].astype(F32), F32),
                ],
                axis=0,
            )
            rings[s] = ring.astype(BF16).reshape(RING, BS, chans)
            copy(rings.at[s], outs[k].at[r], sems.at[s]).start()
    for k in range(columns):
        for r in range(CAP):
            s = k * CAP + r
            copy(rings.at[s], outs[k].at[r], sems.at[s]).wait()


def dispatch_rings(me, experts, owner, fields, north, south, west, east, per, columns):
    height, width, chans = fields.shape
    slots = columns * CAP
    return pl.pallas_call(
        functools.partial(ring_kernel, per, columns),
        out_shape=[jax.ShapeDtypeStruct((CAP, RING, BS, chans), BF16)] * columns,
        in_specs=[whole(pltpu.SMEM)] * 3 + [whole(pltpu.HBM)] + [whole()] * 4,
        out_specs=[whole(pltpu.HBM)] * columns,
        scratch_shapes=[
            pltpu.VMEM((height + 2, width, chans), BF16),
            pltpu.VMEM(((height + 2) * (width + 2 * GAP), chans), F32),
            pltpu.VMEM((slots, RING, BS, chans), BF16),
        ]
        + tables(columns)
        + [pltpu.SemaphoreType.DMA, pltpu.SemaphoreType.DMA((slots,))],
        compiler_params=params(60),
        cost_estimate=pl.CostEstimate(flops=0, bytes_accessed=3_000_000, transcendentals=0),
        name="dispatch_rings",
    )(me, experts, owner, fields, north, south, west, east)


def load_slot(own, ring, column, r, target, sem):
    copy(own.at[column, r], target.at[pl.ds(0, OWN)], sem).start()
    copy(ring.at[r], target.at[pl.ds(OWN, RING)], sem).start()


def shifted_windows(data, wide):
    chans = wide.shape[1]
    ring = data[OWN:LINES].reshape(RING * BS, chans).astype(F32)
    bottom = SPAN * (EDGE - 1)
    wide[7 : 7 + EDGE, :] = ring[0:EDGE]
    wide[bottom + 7 : bottom + 7 + EDGE, :] = ring[EDGE : 2 * EDGE]
    wide[pl.ds(SPAN + 7, BS, stride=SPAN), :] = ring[2 * EDGE : 2 * EDGE + BS]
    wide[pl.ds(SPAN + 8 + BS, BS, stride=SPAN), :] = ring[2 * EDGE + BS : NUMBER]
    for x in range(BS):
        start = SPAN * (x + 1) + 8
        wide[start : start + BS, :] = data[BS + x].astype(F32)
    first = [wide[SPAN * u + 7 : SPAN * u + 7 + BS, :] for u in range(EDGE)]
    third = [wide[SPAN * u + 9 : SPAN * u + 9 + BS, :] for u in range(EDGE)]
    return (
        jnp.concatenate(first, axis=0).astype(BF16),
        jnp.concatenate(
            [
                wide[8 : 8 + BS, :].astype(BF16),
                data[BS:OWN].reshape(CELLS, chans),
                wide[bottom + 8 : bottom + 8 + BS, :].astype(BF16),
            ],
            axis=0,
        ),
        jnp.concatenate(third, axis=0).astype(BF16),
    )


def nine_taps(windows):
    return jnp.concatenate(
        [w[BS * a : BS * a + CELLS] for a in range(3) for w in windows], axis=1
    )


def load_banks(place, banks, held, sems, slots, size):
    for s in range(slots):
        piece = lax.div(place[s], size)
        row = lax.rem(place[s], size)
        p = 0
        for bank in banks:
            for start in range(0, bank.shape[0], size):

                @pl.when(piece == p)
                def _():
                    copy(bank.at[start + row], held.at[s], sems.at[s]).start()

                p += 1


def taps_kernel(size, columns, pieces, extras, me, place, own, *refs):
    rings, refs = refs[:columns], refs[columns:]
    banks, refs = refs[:pieces], refs[pieces + extras :]
    (out, _, held, stage, result, wide, cots, lines, before, after, bank_sems, load_sems,
     out_sems) = refs
    chans = cots.shape[1]
    slots = CAP * columns
    for k in range(columns):
        for r in range(CAP):
            s = k * CAP + r
            load_slot(own, rings[k], me[0] ^ k, r, stage.at[s], load_sems.at[s])
    load_banks(place, banks, held, bank_sems, slots, size)
    cots[...] = jnp.zeros(cots.shape, F32)
    lines[...] = jnp.zeros(lines.shape, BF16)
    before[...] = jnp.zeros(before.shape, F32)
    after[...] = jnp.zeros(after.shape, F32)

    def visit(s, carry):
        copy(stage.at[s], stage.at[s], load_sems.at[s]).wait()
        copy(held.at[s], held.at[s], bank_sems.at[s]).wait()
        data = stage.at[s]
        bank = held.at[s]
        for x in range(BS):
            cots[SPAN * x + 8 : SPAN * x + 8 + BS, :] = data[x].astype(F32)
            lines[1, BS * (x + 2) : BS * (x + 3), :] = data[x]
        for x in range(BS):
            lines[0, BS * (x + 2) : BS * (x + 3), :] = cots[
                SPAN * x + 9 : SPAN * x + 9 + BS, :
            ].astype(BF16)
            lines[2, BS * (x + 2) : BS * (x + 3), :] = cots[
                SPAN * x + 7 : SPAN * x + 7 + BS, :
            ].astype(BF16)
        before[2 : 2 + BS, :] = cots[pl.ds(8, BS, stride=SPAN), :]
        after[EDGE + 2 : EDGE + 2 + BS, :] = cots[pl.ds(8 + BS - 1, BS, stride=SPAN), :]
        sides = []
        for a in range(3):
            for b in range(3):
                if b == 0:
                    tail = before[2 - a : 2 - a + TAIL, :].astype(BF16)
                elif b == 2:
                    tail = after[2 - a : 2 - a + TAIL, :].astype(BF16)
                else:
                    tail = jnp.zeros((TAIL, chans), BF16)
                main = lines[b, (2 - a) * BS : (2 - a) * BS + MAIN, :]
                sides.append(jnp.concatenate([main, tail], axis=0))
        spread = lax.dot_general(
            jnp.concatenate(sides, axis=1),
            jnp.concatenate([bank[t] for t in range(9)], axis=1),
            (((1,), (1,)), ((), ())),
            preferred_element_type=F32,
        )
        result[s, BS:] = spread.astype(BF16).reshape(WINDOW, BS, chans)
        output = jnp.dot(
            nine_taps(shifted_windows(data, wide)),
            bank[...].reshape(9 * chans, chans),
            preferred_element_type=F32,
        )
        result[s, 0:BS] = output.astype(BF16).reshape(BS, BS, chans)
        target = out.at[me[0] ^ lax.div(s, CAP), lax.rem(s, CAP)]
        copy(result.at[s], target, out_sems.at[s]).start()
        return carry

    lax.fori_loop(0, slots, visit, 0)
    for s in range(slots):
        copy(result.at[s], result.at[s], out_sems.at[s]).wait()


def taps(me, place, own, rings, banks, after):
    columns, chans = len(rings), own.shape[-1]
    slots = CAP * columns
    size = min(bank.shape[0] for bank in banks)
    inputs = [me, place, own] + list(rings) + list(banks) + list(after)
    return pl.pallas_call(
        functools.partial(taps_kernel, size, columns, len(banks), len(after)),
        out_shape=[
            jax.ShapeDtypeStruct((columns, CAP, BACK, BS, chans), BF16),
            TOKEN,
        ],
        in_specs=[whole(pltpu.SMEM)] * 2
        + [whole(pltpu.HBM)] * (len(inputs) - 2),
        out_specs=[whole(pltpu.HBM)] * 2,
        scratch_shapes=[
            pltpu.VMEM((slots,) + banks[0].shape[1:], BF16),
            pltpu.VMEM((slots, LINES, BS, chans), BF16),
            pltpu.VMEM((slots, BACK, BS, chans), BF16),
            pltpu.VMEM((EDGE * SPAN, chans), F32),
            pltpu.VMEM((EDGE * SPAN, chans), F32),
            pltpu.VMEM((3, (BS + 4) * BS, chans), BF16),
            pltpu.VMEM((TAIL + 8, chans), F32),
            pltpu.VMEM((TAIL + 8, chans), F32),
        ]
        + [pltpu.SemaphoreType.DMA((slots,))] * 3,
        compiler_params=params(60),
        cost_estimate=pl.CostEstimate(
            flops=175_000_000 * slots, bytes_accessed=600_000 * slots, transcendentals=0
        ),
        name="taps",
    )(*inputs)


def grads_kernel(piece, per, columns, terms, extras, me, place, own, *refs):
    rings, refs = refs[:columns], refs[columns:]
    added, refs = refs[:terms], refs[terms + extras :]
    (out, _, stage, extra, total, wide, result, seen, load_sems, extra_sems,
     out_sems) = refs
    slots = CAP * columns
    chans = wide.shape[1]
    for k in range(columns):
        for r in range(CAP):
            s = k * CAP + r

            @pl.when(lax.div(place[s], per) == piece)
            def _():
                load_slot(own, rings[k], me[0] ^ k, r, stage.at[s], load_sems.at[s])

    for j in range(per):
        seen[j] = 0
        for i, term in enumerate(added):
            copy(term.at[j], extra.at[i, j], extra_sems.at[i * per + j]).start()

    def visit(s, carry):
        index = place[s]

        @pl.when(lax.div(index, per) == piece)
        def _():
            j = lax.rem(index, per)
            copy(stage.at[s], stage.at[s], load_sems.at[s]).wait()
            data = stage.at[s]
            term = lax.dot_general(
                data[0:BS].reshape(CELLS, chans),
                nine_taps(shifted_windows(data, wide)),
                (((0,), (0,)), ((), ())),
                preferred_element_type=F32,
            )

            @pl.when(seen[j] == 0)
            def _():
                total[j] = term

            @pl.when(seen[j] > 0)
            def _():
                total[j] += term

            seen[j] = 1

        return carry

    lax.fori_loop(0, slots, visit, 0)

    def expert(j, carry):
        for i in range(terms):
            copy(extra.at[i, j], extra.at[i, j], extra_sems.at[i * per + j]).wait()

        @pl.when(seen[j] > 0)
        def _():
            value = total[j]
            for i in range(terms):
                value = value + extra[i, j].astype(F32)
            result[j] = value.astype(result.dtype)

        @pl.when(seen[j] == 0)
        def _():
            value = jnp.zeros(result.shape[1:], F32)
            for i in range(terms):
                value = value + extra[i, j].astype(F32)
            result[j] = value.astype(result.dtype)

        copy(result.at[j], out.at[j], out_sems.at[j]).start()
        return carry

    lax.fori_loop(0, per, expert, 0)
    for j in range(per):
        copy(result.at[j], out.at[j], out_sems.at[j]).wait()


def grads(me, place, own, rings, piece, bank_shape, added, after, dtype):
    per, taps_n, chans, outs = bank_shape
    columns = len(rings)
    slots = CAP * columns
    terms = max(len(added), 1)
    shape = (per, outs, taps_n * chans)
    inputs = [me, place, own] + list(rings) + list(added) + list(after)
    return pl.pallas_call(
        functools.partial(grads_kernel, piece, per, columns, len(added), len(after)),
        out_shape=[jax.ShapeDtypeStruct(shape, dtype), TOKEN],
        in_specs=[whole(pltpu.SMEM)] * 2
        + [whole(pltpu.HBM)] * (len(inputs) - 2),
        out_specs=[whole(pltpu.HBM)] * 2,
        scratch_shapes=[
            pltpu.VMEM((slots, LINES, BS, chans), BF16),
            pltpu.VMEM((terms, per if added else 1) + shape[1:], BF16),
            pltpu.VMEM(shape, F32),
            pltpu.VMEM((EDGE * SPAN, chans), F32),
            pltpu.VMEM(shape, dtype),
            pltpu.SMEM((per,), jnp.int32),
            pltpu.SemaphoreType.DMA((slots,)),
            pltpu.SemaphoreType.DMA((terms * per,)),
            pltpu.SemaphoreType.DMA((per,)),
        ],
        compiler_params=params(60),
        cost_estimate=pl.CostEstimate(
            flops=300_000_000, bytes_accessed=6_000_000, transcendentals=0
        ),
        name="grads",
    )(*inputs)


def bank_kernel(count, *refs):
    terms, refs = refs[:count], refs[count:]
    out = refs[0]
    stages, refs = refs[2 : count + 2], refs[count + 2 :]
    result, load_sems, out_sems = refs
    per, taps_n, chans, outs = out.shape
    for j in range(per):
        for i, (term, stage) in enumerate(zip(terms, stages)):
            copy(term.at[j], stage.at[j], load_sems.at[i * per + j]).start()

    def expert(j, carry):
        for i, stage in enumerate(stages):
            copy(stage.at[j], stage.at[j], load_sems.at[i * per + j]).wait()
        for t in range(taps_n):
            columns = slice(t * chans, (t + 1) * chans)
            value = stages[0][j, :, columns].astype(F32)
            for stage in stages[1:]:
                value = value + stage[j, :, columns].astype(F32)
            result[j, t] = value.T
        copy(result.at[j], out.at[j], out_sems.at[j]).start()
        return carry

    lax.fori_loop(0, per, expert, 0)
    for j in range(per):
        copy(result.at[j], out.at[j], out_sems.at[j]).wait()


def bank_of(terms, bank_shape):
    per = bank_shape[0]
    return pl.pallas_call(
        functools.partial(bank_kernel, len(terms)),
        out_shape=[jax.ShapeDtypeStruct(bank_shape, F32), TOKEN],
        in_specs=[whole(pltpu.HBM)] * len(terms),
        out_specs=[whole(pltpu.HBM)] * 2,
        scratch_shapes=[pltpu.VMEM(term.shape, term.dtype) for term in terms]
        + [
            pltpu.VMEM(bank_shape, F32),
            pltpu.SemaphoreType.DMA((len(terms) * per,)),
            pltpu.SemaphoreType.DMA((per,)),
        ],
        compiler_params=params(24),
        cost_estimate=pl.CostEstimate(flops=0, bytes_accessed=12_000_000, transcendentals=0),
        name="bank",
    )(*terms)


def canvas_kernel(per, columns, shape, extras, experts, owner, source, *refs):
    refs = refs[extras:]
    canvas, north, south, west, east, blocks, numbers, counts = refs
    height, width, chans = shape
    stride = width + 2 * GAP
    plan_slots(experts, owner, blocks, numbers, counts, per, columns)

    def clear(r, carry):
        start = pl.multiple_of(r * stride, 8)
        canvas[pl.ds(start, stride), :] = jnp.zeros((stride, chans), F32)
        return carry

    lax.fori_loop(0, height + 2, clear, 0)

    def visit(s, carry):
        data = source.at[lax.div(s, CAP), lax.rem(s, CAP)]
        held = blocks[s]

        @pl.when(held >= 0)
        def _():
            top, left = corner(held, experts.shape[1])
            for u in range(EDGE):
                place = pl.ds(pl.multiple_of((top + u) * stride + GAP + left, 8), BS)
                canvas[place, :] = canvas[place, :] + data[BS + u].astype(F32)
            tail = data[BS + EDGE : BACK].reshape(TAIL, chans).astype(F32)
            start = top * stride + left
            place = pl.ds(start + GAP - 1, EDGE, stride=stride)
            canvas[place, :] = canvas[place, :] + tail[0:EDGE]
            place = pl.ds(start + GAP + BS, EDGE, stride=stride)
            canvas[place, :] = canvas[place, :] + tail[EDGE : 2 * EDGE]

        return carry

    lax.fori_loop(0, columns * CAP, visit, 0)
    north[...] = canvas[0:stride, :].astype(BF16)
    south[...] = canvas[(height + 1) * stride : (height + 2) * stride, :].astype(BF16)
    west[...] = canvas[pl.ds(stride + GAP - 1, height, stride=stride), :]
    east[...] = canvas[pl.ds(stride + GAP + width, height, stride=stride), :]


def canvas_of(experts, owner, source, after, shape, per):
    height, width, chans = shape
    columns = source.shape[0]
    stride = width + 2 * GAP
    return pl.pallas_call(
        functools.partial(canvas_kernel, per, columns, shape, len(after)),
        out_shape=(
            jax.ShapeDtypeStruct(((height + 2) * stride, chans), F32),
            jax.ShapeDtypeStruct((stride, chans), BF16),
            jax.ShapeDtypeStruct((stride, chans), BF16),
            jax.ShapeDtypeStruct((height, chans), F32),
            jax.ShapeDtypeStruct((height, chans), F32),
        ),
        in_specs=[whole(pltpu.SMEM)] * 2
        + [whole()]
        + [whole(pltpu.HBM)] * len(after),
        out_specs=(whole(),) * 5,
        scratch_shapes=tables(columns),
        compiler_params=params(16),
        cost_estimate=pl.CostEstimate(flops=0, bytes_accessed=6_000_000, transcendentals=0),
        name="canvas",
    )(experts, owner, source, *after)


def outputs_kernel(per, columns, experts, owner, source, out, _, blocks, numbers, counts, sems):
    plan_slots(experts, owner, blocks, numbers, counts, per, columns)
    for wait in (False, True):
        for s in range(columns * CAP):
            held = blocks[s]

            @pl.when(held >= 0)
            def _():
                top, left = corner(held, experts.shape[1])
                target = out.at[pl.ds(top, BS), pl.ds(left, BS), :]
                move = copy(source.at[s // CAP, s % CAP, pl.ds(0, BS)], target, sems.at[s])
                if wait:
                    move.wait()
                else:
                    move.start()


def outputs_of(experts, owner, source, shape, per):
    columns = source.shape[0]
    return pl.pallas_call(
        functools.partial(outputs_kernel, per, columns),
        out_shape=[jax.ShapeDtypeStruct(shape, BF16), TOKEN],
        in_specs=[whole(pltpu.SMEM)] * 2 + [whole()],
        out_specs=[whole(pltpu.HBM)] * 2,
        scratch_shapes=tables(columns) + [pltpu.SemaphoreType.DMA((columns * CAP,))],
        compiler_params=params(16),
        cost_estimate=pl.CostEstimate(flops=0, bytes_accessed=3_000_000, transcendentals=0),
        name="outputs",
    )(experts, owner, source)


def finish_kernel(canvas, north, south, west, east, _, out):
    height, width, chans = out.shape
    stride = width + 2 * GAP
    column = lax.broadcasted_iota(jnp.int32, (BS, chans), 0)
    for r in range(height):
        start = (r + 1) * stride + GAP
        line = canvas[start : start + width, :]
        if r == 0:
            line = line + north[GAP : GAP + width, :].astype(F32)
        if r == height - 1:
            line = line + south[GAP : GAP + width, :].astype(F32)
        first = line[:BS] + jnp.where(column == 0, west[r : r + 1, :].astype(F32), 0.0)
        last = line[width - BS :] + jnp.where(
            column == BS - 1, east[r : r + 1, :].astype(F32), 0.0
        )
        out[r] = jnp.concatenate([first, line[BS : width - BS], last], axis=0).astype(BF16)


def finish(canvas, north, south, west, east, after, shape):
    return pl.pallas_call(
        finish_kernel,
        out_shape=jax.ShapeDtypeStruct(shape, BF16),
        in_specs=[whole()] * 5 + [whole(pltpu.HBM)],
        out_specs=whole(),
        compiler_params=params(16),
        cost_estimate=pl.CostEstimate(flops=0, bytes_accessed=4_000_000, transcendentals=0),
        name="finish",
    )(canvas, north, south, west, east, after)


def across(array, axis, shift, wrap):
    count = lax.axis_size(axis)
    pairs = [(i, i + shift) for i in range(count)]
    if wrap:
        pairs = [(i, j % count) for i, j in pairs]
    else:
        pairs = [(i, j) for i, j in pairs if 0 <= j < count]
    return lax.ppermute(array, axis, pairs)


def to_other_core(array):
    return lax.ppermute(array, "lat", [(i, i ^ 1) for i in range(lax.axis_size("lat"))])


def to_chip(array, shift):
    count = lax.axis_size("lat")
    return lax.ppermute(array, "lat", [(i, (i + 2 * shift) % count) for i in range(count)])


def swap(array, k):
    if k == 0:
        return array
    return lax.ppermute(array, "lon", [(i, i ^ k) for i in range(lax.axis_size("lon"))])


def exchange(array):
    return lax.all_to_all(array, "lon", split_axis=0, concat_axis=0, tiled=True)


def tied(arrays, others):
    return lax.optimization_barrier((arrays, others))[0]


def places_of(rings, chips, per):
    lat_index = lax.axis_index("lat")
    line, row = NUMBER // BS, NUMBER % BS
    numbers = jnp.concatenate([ring[:, line, row, 0] for ring in rings]).astype(jnp.int32)
    owner_lat = numbers // per
    chip_step = (owner_lat // 2 - lat_index // 2 + chips) % chips
    core_step = (owner_lat % 2 - lat_index % 2 + 2) % 2
    return (2 * chip_step + core_step) * per + numbers % per


def local(fields, cotangent, kernel_bank, block_expert, owner):
    columns = lax.axis_size("lon")
    chips = lax.axis_size("lat") // 2
    per = kernel_bank.shape[0]
    shape = kernel_bank.shape
    me = lax.axis_index("lon").astype(jnp.int32).reshape(1)

    north = across(fields[-1:], "lat", 1, False)
    south = across(fields[:1], "lat", -1, False)
    first, last = rims_of(
        north, south, fields[:, 0].astype(F32), fields[:, -1].astype(F32)
    )
    west = across(last, "lon", 1, True)
    east = across(first, "lon", -1, True)
    own = dispatch_own(block_expert, owner, fields, cotangent, per, columns)
    own = exchange(tied(own, (west, east)))

    rings = dispatch_rings(
        me, block_expert, owner, fields, north, south, west, east, per, columns
    )
    rings = [swap(array, k) for k, array in enumerate(rings)]
    stored = tied(kernel_bank, (west, east))
    banks = [kernel_bank, to_other_core(stored)]
    for k in range(1, chips):
        distant = tied(to_chip(stored, -k), rings[1 : columns // 2])
        banks += [distant, to_other_core(distant)]

    place = places_of(rings, chips, per)
    slots = (me, place, own, rings)

    results, taps_token = taps(*slots, banks, [])
    results = exchange(results)

    arrived, tokens = [], [taps_token]
    for k in range(1, chips):
        part, token = grads(*slots, 2 * k + 1, shape, [], tokens, BF16)
        part, token = grads(*slots, 2 * k, shape, [to_other_core(part)], [token], BF16)
        arrived.append(to_chip(part, k))
        tokens = [token]
    core_part, core_token = grads(*slots, 1, shape, [], tokens, BF16)
    own_part, own_token = grads(*slots, 0, shape, [], tokens, F32)
    arrived.append(to_other_core(core_part))

    canvas, top, bottom, left, right = canvas_of(
        block_expert, owner, results, [core_token, own_token], fields.shape, per
    )
    above = across(bottom, "lat", 1, False)
    below = across(top, "lat", -1, False)
    outputs, token = outputs_of(block_expert, owner, results, fields.shape, per)
    left, right = corners_of(above, below, left, right, token)
    from_west = across(right, "lon", 1, True)
    from_east = across(left, "lon", -1, True)
    grad_bank, token = bank_of([own_part] + arrived, shape)
    grad_fields = finish(canvas, above, below, from_west, from_east, token, fields.shape)
    return (outputs, grad_fields, grad_bank)


def solution(mesh):
    return jax.shard_map(
        local,
        mesh=mesh,
        in_specs=(
            P("lat", "lon", None),
            P("lat", "lon", None),
            P(("lat", "lon"), None, None, None),
            P("lat", "lon"),
            P(),
        ),
        out_specs=(
            P("lat", "lon", None),
            P("lat", "lon", None),
            P(("lat", "lon"), None, None, None),
        ),
        check_vma=False,
    )
```

```python
import functools

import jax
import jax.numpy as jnp
from jax import lax
from jax.experimental import pallas as pl
from jax.experimental.pallas import tpu as pltpu
from jax.sharding import PartitionSpec as P

BS = 16
CAP = 2
EDGE = BS + 2
CELLS = BS * BS
MAIN = EDGE * BS
TAIL = 48
OWN = 2 * BS
RING = 5
LINES = OWN + RING
NUMBER = 4 * BS + 4
WINDOW = EDGE + TAIL // BS
BACK = BS + WINDOW
GAP = 8
SPAN = 2 * BS
GRANT = 59
F32 = jnp.float32
BF16 = jnp.bfloat16


def params(mib):
    return pltpu.CompilerParams(vmem_limit_bytes=mib * 1024 * 1024)


TOKEN = jax.ShapeDtypeStruct((8, 128), jnp.float32)


def whole(memory=pltpu.VMEM):
    return pl.BlockSpec(memory_space=memory)


def copy(source, target, sem):
    return pltpu.make_async_copy(source, target, sem)


def corner(block, lon_blocks):
    top = lax.div(block, lon_blocks) * BS
    return top, pl.multiple_of(lax.rem(block, lon_blocks) * BS, BS)


def tables(columns):
    return [
        pltpu.SMEM((columns * CAP,), jnp.int32),
        pltpu.SMEM((columns * CAP,), jnp.int32),
        pltpu.SMEM((columns,), jnp.int32),
    ]


def plan_slots(experts, owner, blocks, numbers, counts, per, columns):
    lat_blocks, lon_blocks = experts.shape

    def clear_slot(s, carry):
        blocks[s] = -1
        numbers[s] = 0
        return carry

    def clear_count(s, carry):
        counts[s] = 0
        return carry

    lax.fori_loop(0, columns * CAP, clear_slot, 0)
    lax.fori_loop(0, columns, clear_count, 0)

    def place(b, carry):
        stored = owner[experts[lax.div(b, lon_blocks), lax.rem(b, lon_blocks)]]
        group = lax.div(stored, per)
        column = lax.rem(group, columns)
        rank = counts[column]
        counts[column] = rank + 1
        slot = column * CAP + rank
        blocks[slot] = b
        numbers[slot] = lax.div(group, columns) * per + lax.rem(stored, per)
        return carry

    lax.fori_loop(0, lat_blocks * lon_blocks, place, 0)


def own_kernel(per, columns, experts, owner, fields, cot, *refs):
    out, _, grid, cells, blank, blocks, numbers, counts, load_sems, sems = refs
    height, width, chans = fields.shape
    sources = (cells, grid)
    loads = [copy(cot, cells, load_sems.at[0]), copy(fields, grid, load_sems.at[1])]
    for load in loads:
        load.start()
    plan_slots(experts, owner, blocks, numbers, counts, per, columns)
    blank[...] = jnp.zeros(blank.shape, BF16)
    for part, source in enumerate(sources):
        loads[part].wait()
        for column in range(columns):
            for r in range(CAP):
                s = column * CAP + r
                held = blocks[s]
                top, left = corner(jnp.maximum(held, 0), experts.shape[1])
                target = out.at[column, r, pl.ds(part * BS, BS)]

                @pl.when(held >= 0)
                def _():
                    copy(
                        source.at[pl.ds(top, BS), pl.ds(left, BS), :], target, sems.at[part, s]
                    ).start()

                @pl.when(held < 0)
                def _():
                    copy(blank, target, sems.at[part, s]).start()

    for part in range(2):
        for s in range(columns * CAP):
            copy(blank, out.at[0, 0, pl.ds(0, BS)], sems.at[part, s]).wait()


def dispatch_own(experts, owner, fields, cot, per, columns):
    chans = cot.shape[2]
    out = pl.pallas_call(
        functools.partial(own_kernel, per, columns),
        out_shape=[
            jax.ShapeDtypeStruct((columns, CAP, LINES, BS, chans), BF16),
            TOKEN,
        ],
        in_specs=[whole(pltpu.SMEM)] * 2 + [whole(pltpu.HBM)] * 2,
        out_specs=[whole(pltpu.HBM)] * 2,
        scratch_shapes=[
            pltpu.VMEM(fields.shape, BF16),
            pltpu.VMEM(cot.shape, BF16),
            pltpu.VMEM((BS, BS, chans), BF16),
        ]
        + tables(columns)
        + [pltpu.SemaphoreType.DMA((2,)), pltpu.SemaphoreType.DMA((2, columns * CAP))],
        compiler_params=params(GRANT),
        cost_estimate=pl.CostEstimate(flops=0, bytes_accessed=6_000_000, transcendentals=0),
        name="dispatch_own",
    )(experts, owner, fields, cot)
    return out


def rims_kernel(north, south, first, last, first_out, last_out):
    width = north.shape[1]
    for inner, out, left, column in (
        (first, first_out, 0, 0),
        (last, last_out, width - BS, BS - 1),
    ):
        above = north[0, left : left + BS, :].astype(F32)
        below = south[0, left : left + BS, :].astype(F32)
        out[...] = jnp.concatenate(
            [above[column : column + 1], inner[...], below[column : column + 1]], axis=0
        ).astype(BF16)


def rims_of(north, south, first, last):
    height, chans = first.shape
    return pl.pallas_call(
        rims_kernel,
        out_shape=[jax.ShapeDtypeStruct((height + 2, chans), BF16)] * 2,
        in_specs=[whole()] * 4,
        out_specs=[whole()] * 2,
        compiler_params=params(4),
        name="rims",
    )(north, south, first, last)


def corners_kernel(above, below, left, right, _, left_out, right_out):
    height = left.shape[0]
    row = lax.broadcasted_iota(jnp.int32, left.shape, 0)
    stride = above.shape[0]
    for line, out, start, column in (
        (left, left_out, 0, GAP - 1),
        (right, right_out, stride - BS, BS - GAP),
    ):
        top = above[start : start + BS, :].astype(F32)[column : column + 1]
        bottom = below[start : start + BS, :].astype(F32)[column : column + 1]
        out[...] = (
            line[...]
            + jnp.where(row == 0, top, 0.0)
            + jnp.where(row == height - 1, bottom, 0.0)
        ).astype(BF16)


def corners_of(above, below, left, right, after):
    return pl.pallas_call(
        corners_kernel,
        out_shape=[jax.ShapeDtypeStruct(left.shape, BF16)] * 2,
        in_specs=[whole()] * 4 + [whole(pltpu.HBM)],
        out_specs=[whole()] * 2,
        compiler_params=params(4),
        name="corners",
    )(above, below, left, right, after)


def ring_kernel(
    per, columns, experts, owner, fields, north, south, west, east, _, out, rows, wide, rings,
    blocks, numbers, counts, load_sem, sems,
):
    height, width, chans = fields.shape
    stride = width + 2 * GAP
    load = copy(fields, rows.at[pl.ds(1, height)], load_sem)
    load.start()
    plan_slots(experts, owner, blocks, numbers, counts, per, columns)
    rows[0] = north[0]
    rows[height + 1] = south[0]
    load.wait()

    def widen(r, carry):
        start = pl.multiple_of(r * stride + GAP, 8)
        wide[pl.ds(start, width), :] = rows[r].astype(F32)
        return carry

    lax.fori_loop(0, height + 2, widen, 0)
    wide[pl.ds(GAP - 1, height + 2, stride=stride), :] = west[...].astype(F32)
    wide[pl.ds(GAP + width, height + 2, stride=stride), :] = east[...].astype(F32)
    for s in range(columns * CAP):
        top, left = corner(jnp.maximum(blocks[s], 0), experts.shape[1])
        start = pl.multiple_of(top * stride + left, 8)
        upper = wide[pl.ds(start, BS + 2 * GAP), :]
        start = pl.multiple_of(start + (EDGE - 1) * stride, 8)
        lower = wide[pl.ds(start, BS + 2 * GAP), :]
        start = (top + 1) * stride + left
        ring = jnp.concatenate(
            [
                upper[GAP - 1 : GAP + BS + 1],
                lower[GAP - 1 : GAP + BS + 1],
                wide[pl.ds(start + GAP - 1, BS, stride=stride), :],
                wide[pl.ds(start + GAP + BS, BS, stride=stride), :],
                jnp.full((RING * BS - NUMBER, chans), numbers[s].astype(F32), F32),
            ],
            axis=0,
        )
        rings[s] = ring.astype(BF16).reshape(RING, BS, chans)
        target = out.at[s // CAP, s % CAP, pl.ds(OWN, RING)]
        copy(rings.at[s], target, sems.at[s]).start()
    for s in range(columns * CAP):
        target = out.at[s // CAP, s % CAP, pl.ds(OWN, RING)]
        copy(rings.at[s], target, sems.at[s]).wait()


def dispatch_rings(experts, owner, fields, north, south, west, east, filled, per):
    height, width, chans = fields.shape
    columns = filled.shape[0]
    slots = columns * CAP
    return pl.pallas_call(
        functools.partial(ring_kernel, per, columns),
        out_shape=jax.ShapeDtypeStruct(filled.shape, BF16),
        in_specs=[whole(pltpu.SMEM)] * 2
        + [whole(pltpu.HBM)]
        + [whole()] * 4
        + [whole(pltpu.HBM)],
        out_specs=whole(pltpu.HBM),
        input_output_aliases={7: 0},
        scratch_shapes=[
            pltpu.VMEM((height + 2, width, chans), BF16),
            pltpu.VMEM(((height + 2) * (width + 2 * GAP), chans), F32),
            pltpu.VMEM((slots, RING, BS, chans), BF16),
        ]
        + tables(columns)
        + [pltpu.SemaphoreType.DMA, pltpu.SemaphoreType.DMA((slots,))],
        compiler_params=params(GRANT),
        cost_estimate=pl.CostEstimate(flops=0, bytes_accessed=3_000_000, transcendentals=0),
        name="dispatch_rings",
    )(experts, owner, fields, north, south, west, east, filled)


def shifted_windows(data, wide):
    chans = wide.shape[1]
    ring = data[OWN:LINES].reshape(RING * BS, chans).astype(F32)
    bottom = SPAN * (EDGE - 1)
    wide[7 : 7 + EDGE, :] = ring[0:EDGE]
    wide[bottom + 7 : bottom + 7 + EDGE, :] = ring[EDGE : 2 * EDGE]
    wide[pl.ds(SPAN + 7, BS, stride=SPAN), :] = ring[2 * EDGE : 2 * EDGE + BS]
    wide[pl.ds(SPAN + 8 + BS, BS, stride=SPAN), :] = ring[2 * EDGE + BS : NUMBER]
    for x in range(BS):
        start = SPAN * (x + 1) + 8
        wide[start : start + BS, :] = data[BS + x].astype(F32)
    first = [wide[SPAN * u + 7 : SPAN * u + 7 + BS, :] for u in range(EDGE)]
    third = [wide[SPAN * u + 9 : SPAN * u + 9 + BS, :] for u in range(EDGE)]
    return (
        jnp.concatenate(first, axis=0).astype(BF16),
        jnp.concatenate(
            [
                wide[8 : 8 + BS, :].astype(BF16),
                data[BS:OWN].reshape(CELLS, chans),
                wide[bottom + 8 : bottom + 8 + BS, :].astype(BF16),
            ],
            axis=0,
        ),
        jnp.concatenate(third, axis=0).astype(BF16),
    )


def nine_taps(windows):
    return jnp.concatenate(
        [w[BS * a : BS * a + CELLS] for a in range(3) for w in windows], axis=1
    )


def load_bank(index, banks, target, sem, size):
    piece = lax.div(index, size)
    row = lax.rem(index, size)
    p = 0
    for bank in banks:
        for start in range(0, bank.shape[0], size):

            @pl.when(piece == p)
            def _():
                copy(bank.at[start + row], target, sem).start()

            p += 1


def taps_kernel(size, per, wanted, pieces, place, slots_in, *refs):
    banks, refs = refs[:pieces], refs[pieces:]
    out, sums, refs = refs[0], refs[1 : len(wanted) + 1], refs[len(wanted) + 1 :]
    (held, stage, result, wide, cots, lines, before, after, total, rounded, seen, bank_sems,
     load_sems, out_sems, sum_sems) = refs
    chans = cots.shape[1]
    slots = CAP * slots_in.shape[0]
    for s in range(slots):
        copy(slots_in.at[s // CAP, s % CAP], stage.at[s], load_sems.at[s]).start()
        load_bank(place[s // CAP, s % CAP], banks, held.at[s], bank_sems.at[s], size)
    for e in range(len(wanted) * per):
        seen[e] = 0
    cots[...] = jnp.zeros(cots.shape, F32)
    lines[...] = jnp.zeros(lines.shape, BF16)
    before[...] = jnp.zeros(before.shape, F32)
    after[...] = jnp.zeros(after.shape, F32)

    def visit(s, carry):
        copy(stage.at[s], stage.at[s], load_sems.at[s]).wait()
        copy(held.at[s], held.at[s], bank_sems.at[s]).wait()
        data = stage.at[s]
        bank = held.at[s]
        for x in range(BS):
            cots[SPAN * x + 8 : SPAN * x + 8 + BS, :] = data[x].astype(F32)
            lines[1, BS * (x + 2) : BS * (x + 3), :] = data[x]
        for x in range(BS):
            lines[0, BS * (x + 2) : BS * (x + 3), :] = cots[
                SPAN * x + 9 : SPAN * x + 9 + BS, :
            ].astype(BF16)
            lines[2, BS * (x + 2) : BS * (x + 3), :] = cots[
                SPAN * x + 7 : SPAN * x + 7 + BS, :
            ].astype(BF16)
        before[2 : 2 + BS, :] = cots[pl.ds(8, BS, stride=SPAN), :]
        after[EDGE + 2 : EDGE + 2 + BS, :] = cots[pl.ds(8 + BS - 1, BS, stride=SPAN), :]
        sides = []
        for a in range(3):
            for b in range(3):
                if b == 0:
                    tail = before[2 - a : 2 - a + TAIL, :].astype(BF16)
                elif b == 2:
                    tail = after[2 - a : 2 - a + TAIL, :].astype(BF16)
                else:
                    tail = jnp.zeros((TAIL, chans), BF16)
                main = lines[b, (2 - a) * BS : (2 - a) * BS + MAIN, :]
                sides.append(jnp.concatenate([main, tail], axis=0))
        spread = lax.dot_general(
            jnp.concatenate(sides, axis=1),
            jnp.concatenate([bank[t] for t in range(9)], axis=1),
            (((1,), (1,)), ((), ())),
            preferred_element_type=F32,
        )
        result[s, BS:] = spread.astype(BF16).reshape(WINDOW, BS, chans)
        windows = nine_taps(shifted_windows(data, wide))
        output = jnp.dot(
            windows,
            bank[...].reshape(9 * chans, chans),
            preferred_element_type=F32,
        )
        result[s, 0:BS] = output.astype(BF16).reshape(BS, BS, chans)
        target = out.at[lax.div(s, CAP), lax.rem(s, CAP)]
        copy(result.at[s], target, out_sems.at[s]).start()
        index = place[lax.div(s, CAP), lax.rem(s, CAP)]
        piece = lax.div(index, per)
        for i, p in enumerate(wanted):

            @pl.when(piece == p)
            def _():
                e = i * per + lax.rem(index, per)
                term = lax.dot_general(
                    data[0:BS].reshape(CELLS, chans),
                    windows,
                    (((0,), (0,)), ((), ())),
                    preferred_element_type=F32,
                )

                @pl.when(seen[e] == 0)
                def _():
                    total[e] = term

                @pl.when(seen[e] > 0)
                def _():
                    total[e] += term

                seen[e] = 1

        return carry

    lax.fori_loop(0, slots, visit, 0)
    for i in range(len(wanted)):

        def expert(j, carry, i=i):
            e = i * per + j

            @pl.when(seen[e] > 0)
            def _():
                rounded[e] = total[e].astype(BF16)

            @pl.when(seen[e] == 0)
            def _():
                rounded[e] = jnp.zeros(rounded.shape[1:], BF16)

            copy(rounded.at[e], sums[i].at[j], sum_sems.at[e]).start()
            return carry

        lax.fori_loop(0, per, expert, 0)
    for s in range(slots):
        copy(result.at[s], result.at[s], out_sems.at[s]).wait()
    for i in range(len(wanted)):
        for j in range(per):
            copy(rounded.at[0], sums[i].at[j], sum_sems.at[i * per + j]).wait()


def taps(place, slots_in, banks, wanted):
    columns, chans = slots_in.shape[0], slots_in.shape[-1]
    slots = CAP * columns
    per, taps_n = banks[0].shape[:2]
    size = min(bank.shape[0] for bank in banks)
    shape = (per, chans, taps_n * chans)
    found = (len(wanted) * per,) + shape[1:]
    out = pl.pallas_call(
        functools.partial(taps_kernel, size, per, wanted, len(banks)),
        out_shape=[jax.ShapeDtypeStruct((columns, CAP, BACK, BS, chans), BF16)]
        + [jax.ShapeDtypeStruct(shape, BF16)] * len(wanted),
        in_specs=[whole(pltpu.SMEM)] + [whole(pltpu.HBM)] * (len(banks) + 1),
        out_specs=[whole(pltpu.HBM)] * (len(wanted) + 1),
        scratch_shapes=[
            pltpu.VMEM((slots,) + banks[0].shape[1:], BF16),
            pltpu.VMEM((slots, LINES, BS, chans), BF16),
            pltpu.VMEM((slots, BACK, BS, chans), BF16),
            pltpu.VMEM((EDGE * SPAN, chans), F32),
            pltpu.VMEM((EDGE * SPAN, chans), F32),
            pltpu.VMEM((3, (BS + 4) * BS, chans), BF16),
            pltpu.VMEM((TAIL + 8, chans), F32),
            pltpu.VMEM((TAIL + 8, chans), F32),
            pltpu.VMEM(found, F32),
            pltpu.VMEM(found, BF16),
            pltpu.SMEM((found[0],), jnp.int32),
        ]
        + [pltpu.SemaphoreType.DMA((slots,))] * 3
        + [pltpu.SemaphoreType.DMA((found[0],))],
        compiler_params=params(GRANT),
        cost_estimate=pl.CostEstimate(
            flops=200_000_000 * slots, bytes_accessed=800_000 * slots, transcendentals=0
        ),
        name="taps",
    )(place, slots_in, *banks)
    return out[0], out[1:]


def grads_kernel(piece, per, terms, extras, place, slots_in, *refs):
    added, refs = refs[:terms], refs[terms + extras :]
    (out, _, stage, extra, total, wide, result, seen, load_sems, extra_sems,
     out_sems) = refs
    slots = CAP * slots_in.shape[0]
    chans = wide.shape[1]
    for s in range(slots):

        @pl.when(lax.div(place[s // CAP, s % CAP], per) == piece)
        def _():
            copy(slots_in.at[s // CAP, s % CAP], stage.at[s], load_sems.at[s]).start()

    for j in range(per):
        seen[j] = 0
        for i, term in enumerate(added):
            copy(term.at[j], extra.at[i, j], extra_sems.at[i * per + j]).start()

    def visit(s, carry):
        index = place[lax.div(s, CAP), lax.rem(s, CAP)]

        @pl.when(lax.div(index, per) == piece)
        def _():
            j = lax.rem(index, per)
            copy(stage.at[s], stage.at[s], load_sems.at[s]).wait()
            data = stage.at[s]
            term = lax.dot_general(
                data[0:BS].reshape(CELLS, chans),
                nine_taps(shifted_windows(data, wide)),
                (((0,), (0,)), ((), ())),
                preferred_element_type=F32,
            )

            @pl.when(seen[j] == 0)
            def _():
                total[j] = term

            @pl.when(seen[j] > 0)
            def _():
                total[j] += term

            seen[j] = 1

        return carry

    lax.fori_loop(0, slots, visit, 0)

    def expert(j, carry):
        for i in range(terms):
            copy(extra.at[i, j], extra.at[i, j], extra_sems.at[i * per + j]).wait()

        @pl.when(seen[j] > 0)
        def _():
            value = total[j]
            for i in range(terms):
                value = value + extra[i, j].astype(F32)
            result[j] = value.astype(result.dtype)

        @pl.when(seen[j] == 0)
        def _():
            value = jnp.zeros(result.shape[1:], F32)
            for i in range(terms):
                value = value + extra[i, j].astype(F32)
            result[j] = value.astype(result.dtype)

        copy(result.at[j], out.at[j], out_sems.at[j]).start()
        return carry

    lax.fori_loop(0, per, expert, 0)
    for j in range(per):
        copy(result.at[j], out.at[j], out_sems.at[j]).wait()


def grads(place, slots_in, piece, bank_shape, added, after, dtype):
    per, taps_n, chans, outs = bank_shape
    slots = CAP * slots_in.shape[0]
    terms = max(len(added), 1)
    shape = (per, outs, taps_n * chans)
    inputs = [place, slots_in] + list(added) + list(after)
    return pl.pallas_call(
        functools.partial(grads_kernel, piece, per, len(added), len(after)),
        out_shape=[jax.ShapeDtypeStruct(shape, dtype), TOKEN],
        in_specs=[whole(pltpu.SMEM)] + [whole(pltpu.HBM)] * (len(inputs) - 1),
        out_specs=[whole(pltpu.HBM)] * 2,
        scratch_shapes=[
            pltpu.VMEM((slots, LINES, BS, chans), BF16),
            pltpu.VMEM((terms, per if added else 1) + shape[1:], BF16),
            pltpu.VMEM(shape, F32),
            pltpu.VMEM((EDGE * SPAN, chans), F32),
            pltpu.VMEM(shape, dtype),
            pltpu.SMEM((per,), jnp.int32),
            pltpu.SemaphoreType.DMA((slots,)),
            pltpu.SemaphoreType.DMA((terms * per,)),
            pltpu.SemaphoreType.DMA((per,)),
        ],
        compiler_params=params(GRANT),
        cost_estimate=pl.CostEstimate(
            flops=300_000_000, bytes_accessed=6_000_000, transcendentals=0
        ),
        name="grads",
    )(*inputs)


def bank_kernel(count, *refs):
    terms, refs = refs[:count], refs[count:]
    out = refs[0]
    stages, refs = refs[2 : count + 2], refs[count + 2 :]
    result, load_sems, out_sems = refs
    per, taps_n, chans, outs = out.shape
    for j in range(per):
        for i, (term, stage) in enumerate(zip(terms, stages)):
            copy(term.at[j], stage.at[j], load_sems.at[i * per + j]).start()

    def expert(j, carry):
        for i, stage in enumerate(stages):
            copy(stage.at[j], stage.at[j], load_sems.at[i * per + j]).wait()
        for t in range(taps_n):
            columns = slice(t * chans, (t + 1) * chans)
            value = stages[0][j, :, columns].astype(F32)
            for stage in stages[1:]:
                value = value + stage[j, :, columns].astype(F32)
            result[j, t] = value.T
        copy(result.at[j], out.at[j], out_sems.at[j]).start()
        return carry

    lax.fori_loop(0, per, expert, 0)
    for j in range(per):
        copy(result.at[j], out.at[j], out_sems.at[j]).wait()


def bank_of(terms, bank_shape):
    per = bank_shape[0]
    return pl.pallas_call(
        functools.partial(bank_kernel, len(terms)),
        out_shape=[jax.ShapeDtypeStruct(bank_shape, F32), TOKEN],
        in_specs=[whole(pltpu.HBM)] * len(terms),
        out_specs=[whole(pltpu.HBM)] * 2,
        scratch_shapes=[pltpu.VMEM(term.shape, term.dtype) for term in terms]
        + [
            pltpu.VMEM(bank_shape, F32),
            pltpu.SemaphoreType.DMA((len(terms) * per,)),
            pltpu.SemaphoreType.DMA((per,)),
        ],
        compiler_params=params(24),
        cost_estimate=pl.CostEstimate(flops=0, bytes_accessed=12_000_000, transcendentals=0),
        name="bank",
    )(*terms)


def canvas_kernel(per, columns, shape, extras, experts, owner, source, *refs):
    refs = refs[extras:]
    canvas, north, south, west, east, blocks, numbers, counts = refs
    height, width, chans = shape
    stride = width + 2 * GAP
    plan_slots(experts, owner, blocks, numbers, counts, per, columns)

    def clear(r, carry):
        start = pl.multiple_of(r * stride, 8)
        canvas[pl.ds(start, stride), :] = jnp.zeros((stride, chans), F32)
        return carry

    lax.fori_loop(0, height + 2, clear, 0)

    def visit(s, carry):
        data = source.at[lax.div(s, CAP), lax.rem(s, CAP)]
        held = blocks[s]

        @pl.when(held >= 0)
        def _():
            top, left = corner(held, experts.shape[1])
            for u in range(EDGE):
                place = pl.ds(pl.multiple_of((top + u) * stride + GAP + left, 8), BS)
                canvas[place, :] = canvas[place, :] + data[BS + u].astype(F32)
            tail = data[BS + EDGE : BACK].reshape(TAIL, chans).astype(F32)
            start = top * stride + left
            place = pl.ds(start + GAP - 1, EDGE, stride=stride)
            canvas[place, :] = canvas[place, :] + tail[0:EDGE]
            place = pl.ds(start + GAP + BS, EDGE, stride=stride)
            canvas[place, :] = canvas[place, :] + tail[EDGE : 2 * EDGE]

        return carry

    lax.fori_loop(0, columns * CAP, visit, 0)
    north[...] = canvas[0:stride, :].astype(BF16)
    south[...] = canvas[(height + 1) * stride : (height + 2) * stride, :].astype(BF16)
    west[...] = canvas[pl.ds(stride + GAP - 1, height, stride=stride), :]
    east[...] = canvas[pl.ds(stride + GAP + width, height, stride=stride), :]


def canvas_of(experts, owner, source, after, shape, per):
    height, width, chans = shape
    columns = source.shape[0]
    stride = width + 2 * GAP
    return pl.pallas_call(
        functools.partial(canvas_kernel, per, columns, shape, len(after)),
        out_shape=(
            jax.ShapeDtypeStruct(((height + 2) * stride, chans), F32),
            jax.ShapeDtypeStruct((stride, chans), BF16),
            jax.ShapeDtypeStruct((stride, chans), BF16),
            jax.ShapeDtypeStruct((height, chans), F32),
            jax.ShapeDtypeStruct((height, chans), F32),
        ),
        in_specs=[whole(pltpu.SMEM)] * 2
        + [whole()]
        + [whole(pltpu.HBM)] * len(after),
        out_specs=(whole(),) * 5,
        scratch_shapes=tables(columns),
        compiler_params=params(16),
        cost_estimate=pl.CostEstimate(flops=0, bytes_accessed=6_000_000, transcendentals=0),
        name="canvas",
    )(experts, owner, source, *after)


def outputs_kernel(per, columns, experts, owner, source, out, _, blocks, numbers, counts, sems):
    plan_slots(experts, owner, blocks, numbers, counts, per, columns)
    for wait in (False, True):
        for s in range(columns * CAP):
            held = blocks[s]

            @pl.when(held >= 0)
            def _():
                top, left = corner(held, experts.shape[1])
                target = out.at[pl.ds(top, BS), pl.ds(left, BS), :]
                move = copy(source.at[s // CAP, s % CAP, pl.ds(0, BS)], target, sems.at[s])
                if wait:
                    move.wait()
                else:
                    move.start()


def outputs_of(experts, owner, source, shape, per):
    columns = source.shape[0]
    return pl.pallas_call(
        functools.partial(outputs_kernel, per, columns),
        out_shape=[jax.ShapeDtypeStruct(shape, BF16), TOKEN],
        in_specs=[whole(pltpu.SMEM)] * 2 + [whole()],
        out_specs=[whole(pltpu.HBM)] * 2,
        scratch_shapes=tables(columns) + [pltpu.SemaphoreType.DMA((columns * CAP,))],
        compiler_params=params(16),
        cost_estimate=pl.CostEstimate(flops=0, bytes_accessed=3_000_000, transcendentals=0),
        name="outputs",
    )(experts, owner, source)


def finish_kernel(canvas, north, south, west, east, _, out):
    height, width, chans = out.shape
    stride = width + 2 * GAP
    column = lax.broadcasted_iota(jnp.int32, (BS, chans), 0)
    for r in range(height):
        start = (r + 1) * stride + GAP
        line = canvas[start : start + width, :]
        if r == 0:
            line = line + north[GAP : GAP + width, :].astype(F32)
        if r == height - 1:
            line = line + south[GAP : GAP + width, :].astype(F32)
        first = line[:BS] + jnp.where(column == 0, west[r : r + 1, :].astype(F32), 0.0)
        last = line[width - BS :] + jnp.where(
            column == BS - 1, east[r : r + 1, :].astype(F32), 0.0
        )
        out[r] = jnp.concatenate([first, line[BS : width - BS], last], axis=0).astype(BF16)


def finish(canvas, north, south, west, east, after, shape):
    return pl.pallas_call(
        finish_kernel,
        out_shape=jax.ShapeDtypeStruct(shape, BF16),
        in_specs=[whole()] * 5 + [whole(pltpu.HBM)],
        out_specs=whole(),
        compiler_params=params(16),
        cost_estimate=pl.CostEstimate(flops=0, bytes_accessed=4_000_000, transcendentals=0),
        name="finish",
    )(canvas, north, south, west, east, after)


def across(array, axis, shift, wrap):
    count = lax.axis_size(axis)
    pairs = [(i, i + shift) for i in range(count)]
    if wrap:
        pairs = [(i, j % count) for i, j in pairs]
    else:
        pairs = [(i, j) for i, j in pairs if 0 <= j < count]
    return lax.ppermute(array, axis, pairs)


def to_other_core(array):
    return lax.ppermute(array, "lat", [(i, i ^ 1) for i in range(lax.axis_size("lat"))])


def to_chip(array, shift):
    count = lax.axis_size("lat")
    return lax.ppermute(array, "lat", [(i, (i + 2 * shift) % count) for i in range(count)])


def exchange(array):
    return lax.all_to_all(array, "lon", split_axis=0, concat_axis=0, tiled=True)


def tied(arrays, others):
    return lax.optimization_barrier((arrays, others))[0]


def places_of(slots, chips, per):
    lat_index = lax.axis_index("lat")
    line, row = OWN + NUMBER // BS, NUMBER % BS
    numbers = slots[:, :, line, row, 0].astype(jnp.int32)
    owner_lat = numbers // per
    chip_step = (owner_lat // 2 - lat_index // 2 + chips) % chips
    core_step = (owner_lat % 2 - lat_index % 2 + 2) % 2
    return (2 * chip_step + core_step) * per + numbers % per


def local(fields, cotangent, kernel_bank, block_expert, owner):
    columns = lax.axis_size("lon")
    chips = lax.axis_size("lat") // 2
    per = kernel_bank.shape[0]
    shape = kernel_bank.shape

    north = across(fields[-1:], "lat", 1, False)
    south = across(fields[:1], "lat", -1, False)
    filled, _ = dispatch_own(block_expert, owner, fields, cotangent, per, columns)
    first, last = rims_of(
        north, south, fields[:, 0].astype(F32), fields[:, -1].astype(F32)
    )
    west = across(last, "lon", 1, True)
    east = across(first, "lon", -1, True)
    filled = dispatch_rings(
        block_expert, owner, fields, north, south, west, east, filled, per
    )
    arrived = exchange(filled)
    place = places_of(arrived, chips, per)
    slots = (place, arrived)

    banks = [kernel_bank, to_other_core(tied(kernel_bank, (west, east)))]
    for k in range(1, chips):
        distant = to_chip(tied(kernel_bank, (first, last)), -k)
        banks += [distant, to_other_core(distant)]

    results, beside = taps(
        place, arrived, banks, tuple(2 * k + 1 for k in range(1, chips))
    )
    results = exchange(results)
    beside = [to_other_core(part) for part in beside]
    chip_parts, tokens = [], []
    for k in range(1, chips):
        part, token = grads(*slots, 2 * k, shape, [beside[k - 1]], tokens, BF16)
        chip_parts.append(to_chip(part, k))
        tokens = [token]
    core_part, core_token = grads(*slots, 1, shape, [], tokens, BF16)
    own_part, own_token = grads(*slots, 0, shape, [], tokens, F32)
    terms = [own_part, to_other_core(core_part)] + chip_parts

    canvas, top, bottom, left, right = canvas_of(
        block_expert, owner, results, [core_token, own_token], fields.shape, per
    )
    above = across(bottom, "lat", 1, False)
    below = across(top, "lat", -1, False)
    outputs, token = outputs_of(block_expert, owner, results, fields.shape, per)
    left, right = corners_of(above, below, left, right, token)
    from_west = across(right, "lon", 1, True)
    from_east = across(left, "lon", -1, True)
    grad_bank, token = bank_of(terms, shape)
    grad_fields = finish(canvas, above, below, from_west, from_east, token, fields.shape)
    return (outputs, grad_fields, grad_bank)


def solution(mesh):
    return jax.shard_map(
        local,
        mesh=mesh,
        in_specs=(
            P("lat", "lon", None),
            P("lat", "lon", None),
            P(("lat", "lon"), None, None, None),
            P("lat", "lon"),
            P(),
        ),
        out_specs=(
            P("lat", "lon", None),
            P("lat", "lon", None),
            P(("lat", "lon"), None, None, None),
        ),
        check_vma=False,
    )
```

```python
import functools

import jax
import jax.numpy as jnp
from jax import lax
from jax.experimental import pallas as pl
from jax.experimental.pallas import tpu as pltpu
from jax.sharding import PartitionSpec as P

BS = 16
CAP = 2
EDGE = BS + 2
CELLS = BS * BS
MAIN = EDGE * BS
TAIL = 48
OWN = 2 * BS
RING = 5
LINES = OWN + RING
NUMBER = 4 * BS + 4
WINDOW = EDGE + TAIL // BS
BACK = BS + WINDOW
SPARE = 8
GAP = 8
SPAN = 2 * BS
GRANT = 59
F32 = jnp.float32
BF16 = jnp.bfloat16


def params(mib):
    return pltpu.CompilerParams(vmem_limit_bytes=mib * 1024 * 1024)


TOKEN = jax.ShapeDtypeStruct((8, 128), jnp.float32)


def whole(memory=pltpu.VMEM):
    return pl.BlockSpec(memory_space=memory)


def copy(source, target, sem):
    return pltpu.make_async_copy(source, target, sem)


def corner(block, lon_blocks):
    top = lax.div(block, lon_blocks) * BS
    return top, pl.multiple_of(lax.rem(block, lon_blocks) * BS, BS)


def tables(columns):
    return [
        pltpu.SMEM((columns * CAP,), jnp.int32),
        pltpu.SMEM((columns * CAP,), jnp.int32),
        pltpu.SMEM((columns,), jnp.int32),
    ]


def plan_slots(experts, owner, blocks, numbers, counts, per, columns):
    lat_blocks, lon_blocks = experts.shape

    def clear_slot(s, carry):
        blocks[s] = -1
        numbers[s] = 0
        return carry

    def clear_count(s, carry):
        counts[s] = 0
        return carry

    lax.fori_loop(0, columns * CAP, clear_slot, 0)
    lax.fori_loop(0, columns, clear_count, 0)

    def place(b, carry):
        stored = owner[experts[lax.div(b, lon_blocks), lax.rem(b, lon_blocks)]]
        group = lax.div(stored, per)
        column = lax.rem(group, columns)
        rank = counts[column]
        counts[column] = rank + 1
        slot = column * CAP + rank
        blocks[slot] = b
        numbers[slot] = lax.div(group, columns) * per + lax.rem(stored, per)
        return carry

    lax.fori_loop(0, lat_blocks * lon_blocks, place, 0)


def own_kernel(per, columns, experts, owner, fields, cot, *refs):
    out, _, grid, cells, blank, blocks, numbers, counts, load_sems, sems = refs
    height, width, chans = fields.shape
    sources = (cells, grid)
    loads = [copy(cot, cells, load_sems.at[0]), copy(fields, grid, load_sems.at[1])]
    for load in loads:
        load.start()
    plan_slots(experts, owner, blocks, numbers, counts, per, columns)
    blank[...] = jnp.zeros(blank.shape, BF16)
    for part, source in enumerate(sources):
        loads[part].wait()
        for column in range(columns):
            for r in range(CAP):
                s = column * CAP + r
                held = blocks[s]
                top, left = corner(jnp.maximum(held, 0), experts.shape[1])
                target = out.at[column, r, pl.ds(part * BS, BS)]

                @pl.when(held >= 0)
                def _():
                    copy(
                        source.at[pl.ds(top, BS), pl.ds(left, BS), :], target, sems.at[part, s]
                    ).start()

                @pl.when(held < 0)
                def _():
                    copy(blank, target, sems.at[part, s]).start()

    for part in range(2):
        for s in range(columns * CAP):
            copy(blank, out.at[0, 0, pl.ds(0, BS)], sems.at[part, s]).wait()


def dispatch_own(experts, owner, fields, cot, per, columns):
    chans = cot.shape[2]
    out = pl.pallas_call(
        functools.partial(own_kernel, per, columns),
        out_shape=[
            jax.ShapeDtypeStruct((columns, CAP, LINES, BS, chans), BF16),
            TOKEN,
        ],
        in_specs=[whole(pltpu.SMEM)] * 2 + [whole(pltpu.HBM)] * 2,
        out_specs=[whole(pltpu.HBM)] * 2,
        scratch_shapes=[
            pltpu.VMEM(fields.shape, BF16),
            pltpu.VMEM(cot.shape, BF16),
            pltpu.VMEM((BS, BS, chans), BF16),
        ]
        + tables(columns)
        + [pltpu.SemaphoreType.DMA((2,)), pltpu.SemaphoreType.DMA((2, columns * CAP))],
        compiler_params=params(GRANT),
        cost_estimate=pl.CostEstimate(flops=0, bytes_accessed=6_000_000, transcendentals=0),
        name="dispatch_own",
    )(experts, owner, fields, cot)
    return out


def rims_kernel(north, south, first, last, first_out, last_out):
    width = north.shape[1]
    for inner, out, left, column in (
        (first, first_out, 0, 0),
        (last, last_out, width - BS, BS - 1),
    ):
        above = north[0, left : left + BS, :].astype(F32)
        below = south[0, left : left + BS, :].astype(F32)
        out[...] = jnp.concatenate(
            [above[column : column + 1], inner[...], below[column : column + 1]], axis=0
        ).astype(BF16)


def rims_of(north, south, first, last):
    height, chans = first.shape
    return pl.pallas_call(
        rims_kernel,
        out_shape=[jax.ShapeDtypeStruct((height + 2, chans), BF16)] * 2,
        in_specs=[whole()] * 4,
        out_specs=[whole()] * 2,
        compiler_params=params(4),
        name="rims",
    )(north, south, first, last)


def corners_kernel(above, below, left, right, _, left_out, right_out):
    height = left.shape[0]
    row = lax.broadcasted_iota(jnp.int32, left.shape, 0)
    stride = above.shape[0]
    for line, out, start, column in (
        (left, left_out, 0, GAP - 1),
        (right, right_out, stride - BS, BS - GAP),
    ):
        top = above[start : start + BS, :].astype(F32)[column : column + 1]
        bottom = below[start : start + BS, :].astype(F32)[column : column + 1]
        out[...] = (
            line[...]
            + jnp.where(row == 0, top, 0.0)
            + jnp.where(row == height - 1, bottom, 0.0)
        ).astype(BF16)


def corners_of(above, below, left, right, after):
    return pl.pallas_call(
        corners_kernel,
        out_shape=[jax.ShapeDtypeStruct(left.shape, BF16)] * 2,
        in_specs=[whole()] * 4 + [whole(pltpu.HBM)],
        out_specs=[whole()] * 2,
        compiler_params=params(4),
        name="corners",
    )(above, below, left, right, after)


def ring_kernel(
    per, columns, experts, owner, fields, north, south, west, east, _, out, rows, wide, rings,
    blocks, numbers, counts, load_sem, sems,
):
    height, width, chans = fields.shape
    stride = width + 2 * GAP
    load = copy(fields, rows.at[pl.ds(1, height)], load_sem)
    load.start()
    plan_slots(experts, owner, blocks, numbers, counts, per, columns)
    rows[0] = north[0]
    rows[height + 1] = south[0]
    load.wait()

    def widen(r, carry):
        start = pl.multiple_of(r * stride + GAP, 8)
        wide[pl.ds(start, width), :] = rows[r].astype(F32)
        return carry

    lax.fori_loop(0, height + 2, widen, 0)
    wide[pl.ds(GAP - 1, height + 2, stride=stride), :] = west[...].astype(F32)
    wide[pl.ds(GAP + width, height + 2, stride=stride), :] = east[...].astype(F32)
    for s in range(columns * CAP):
        top, left = corner(jnp.maximum(blocks[s], 0), experts.shape[1])
        start = pl.multiple_of(top * stride + left, 8)
        upper = wide[pl.ds(start, BS + 2 * GAP), :]
        start = pl.multiple_of(start + (EDGE - 1) * stride, 8)
        lower = wide[pl.ds(start, BS + 2 * GAP), :]
        start = (top + 1) * stride + left
        ring = jnp.concatenate(
            [
                upper[GAP - 1 : GAP + BS + 1],
                lower[GAP - 1 : GAP + BS + 1],
                wide[pl.ds(start + GAP - 1, BS, stride=stride), :],
                wide[pl.ds(start + GAP + BS, BS, stride=stride), :],
                jnp.full((RING * BS - NUMBER, chans), numbers[s].astype(F32), F32),
            ],
            axis=0,
        )
        rings[s] = ring.astype(BF16).reshape(RING, BS, chans)
        target = out.at[s // CAP, s % CAP, pl.ds(OWN, RING)]
        copy(rings.at[s], target, sems.at[s]).start()
    for s in range(columns * CAP):
        target = out.at[s // CAP, s % CAP, pl.ds(OWN, RING)]
        copy(rings.at[s], target, sems.at[s]).wait()


def dispatch_rings(experts, owner, fields, north, south, west, east, filled, per):
    height, width, chans = fields.shape
    columns = filled.shape[0]
    slots = columns * CAP
    return pl.pallas_call(
        functools.partial(ring_kernel, per, columns),
        out_shape=jax.ShapeDtypeStruct(filled.shape, BF16),
        in_specs=[whole(pltpu.SMEM)] * 2
        + [whole(pltpu.HBM)]
        + [whole()] * 4
        + [whole(pltpu.HBM)],
        out_specs=whole(pltpu.HBM),
        input_output_aliases={7: 0},
        scratch_shapes=[
            pltpu.VMEM((height + 2, width, chans), BF16),
            pltpu.VMEM(((height + SPARE) * (width + 2 * GAP), chans), F32),
            pltpu.VMEM((slots, RING, BS, chans), BF16),
        ]
        + tables(columns)
        + [pltpu.SemaphoreType.DMA, pltpu.SemaphoreType.DMA((slots,))],
        compiler_params=params(GRANT),
        cost_estimate=pl.CostEstimate(flops=0, bytes_accessed=3_000_000, transcendentals=0),
        name="dispatch_rings",
    )(experts, owner, fields, north, south, west, east, filled)


def shifted_windows(data, wide):
    chans = wide.shape[1]
    ring = data[OWN:LINES].reshape(RING * BS, chans).astype(F32)
    bottom = SPAN * (EDGE - 1)
    wide[7 : 7 + EDGE, :] = ring[0:EDGE]
    wide[bottom + 7 : bottom + 7 + EDGE, :] = ring[EDGE : 2 * EDGE]
    wide[pl.ds(SPAN + 7, BS, stride=SPAN), :] = ring[2 * EDGE : 2 * EDGE + BS]
    wide[pl.ds(SPAN + 8 + BS, BS, stride=SPAN), :] = ring[2 * EDGE + BS : NUMBER]
    for x in range(BS):
        start = SPAN * (x + 1) + 8
        wide[start : start + BS, :] = data[BS + x].astype(F32)
    first = [wide[SPAN * u + 7 : SPAN * u + 7 + BS, :] for u in range(EDGE)]
    third = [wide[SPAN * u + 9 : SPAN * u + 9 + BS, :] for u in range(EDGE)]
    return (
        jnp.concatenate(first, axis=0).astype(BF16),
        jnp.concatenate(
            [
                wide[8 : 8 + BS, :].astype(BF16),
                data[BS:OWN].reshape(CELLS, chans),
                wide[bottom + 8 : bottom + 8 + BS, :].astype(BF16),
            ],
            axis=0,
        ),
        jnp.concatenate(third, axis=0).astype(BF16),
    )


def nine_taps(windows):
    return jnp.concatenate(
        [w[BS * a : BS * a + CELLS] for a in range(3) for w in windows], axis=1
    )


def load_bank(index, banks, target, sem, size):
    piece = lax.div(index, size)
    row = lax.rem(index, size)
    p = 0
    for bank in banks:
        for start in range(0, bank.shape[0], size):

            @pl.when(piece == p)
            def _():
                copy(bank.at[start + row], target, sem).start()

            p += 1


def taps_kernel(size, per, wanted, pieces, place, slots_in, *refs):
    banks, refs = refs[:pieces], refs[pieces:]
    out, sums, refs = refs[0], refs[1 : len(wanted) + 1], refs[len(wanted) + 1 :]
    (held, stage, result, wide, cots, lines, before, after, total, rounded, seen, bank_sems,
     load_sems, out_sems, sum_sems) = refs
    chans = cots.shape[1]
    slots = CAP * slots_in.shape[0]
    for s in range(slots):
        copy(slots_in.at[s // CAP, s % CAP], stage.at[s], load_sems.at[s]).start()
        load_bank(place[s // CAP, s % CAP], banks, held.at[s], bank_sems.at[s], size)
    for e in range(len(wanted) * per):
        seen[e] = 0
    cots[...] = jnp.zeros(cots.shape, F32)
    lines[...] = jnp.zeros(lines.shape, BF16)
    before[...] = jnp.zeros(before.shape, F32)
    after[...] = jnp.zeros(after.shape, F32)

    def visit(s, carry):
        copy(stage.at[s], stage.at[s], load_sems.at[s]).wait()
        copy(held.at[s], held.at[s], bank_sems.at[s]).wait()
        data = stage.at[s]
        bank = held.at[s]
        for x in range(BS):
            cots[SPAN * x + 8 : SPAN * x + 8 + BS, :] = data[x].astype(F32)
            lines[1, BS * (x + 2) : BS * (x + 3), :] = data[x]
        for x in range(BS):
            lines[0, BS * (x + 2) : BS * (x + 3), :] = cots[
                SPAN * x + 9 : SPAN * x + 9 + BS, :
            ].astype(BF16)
            lines[2, BS * (x + 2) : BS * (x + 3), :] = cots[
                SPAN * x + 7 : SPAN * x + 7 + BS, :
            ].astype(BF16)
        before[2 : 2 + BS, :] = cots[pl.ds(8, BS, stride=SPAN), :]
        after[EDGE + 2 : EDGE + 2 + BS, :] = cots[pl.ds(8 + BS - 1, BS, stride=SPAN), :]
        sides = []
        for a in range(3):
            for b in range(3):
                if b == 0:
                    tail = before[2 - a : 2 - a + TAIL, :].astype(BF16)
                elif b == 2:
                    tail = after[2 - a : 2 - a + TAIL, :].astype(BF16)
                else:
                    tail = jnp.zeros((TAIL, chans), BF16)
                main = lines[b, (2 - a) * BS : (2 - a) * BS + MAIN, :]
                sides.append(jnp.concatenate([main, tail], axis=0))
        spread = lax.dot_general(
            jnp.concatenate(sides, axis=1),
            jnp.concatenate([bank[t] for t in range(9)], axis=1),
            (((1,), (1,)), ((), ())),
            preferred_element_type=F32,
        )
        result[s, BS:] = spread.astype(BF16).reshape(WINDOW, BS, chans)
        windows = nine_taps(shifted_windows(data, wide))
        output = jnp.dot(
            windows,
            bank[...].reshape(9 * chans, chans),
            preferred_element_type=F32,
        )
        result[s, 0:BS] = output.astype(BF16).reshape(BS, BS, chans)
        target = out.at[lax.div(s, CAP), lax.rem(s, CAP)]
        copy(result.at[s], target, out_sems.at[s]).start()
        index = place[lax.div(s, CAP), lax.rem(s, CAP)]
        piece = lax.div(index, per)
        for i, p in enumerate(wanted):

            @pl.when(piece == p)
            def _():
                e = i * per + lax.rem(index, per)
                term = lax.dot_general(
                    data[0:BS].reshape(CELLS, chans),
                    windows,
                    (((0,), (0,)), ((), ())),
                    preferred_element_type=F32,
                )

                @pl.when(seen[e] == 0)
                def _():
                    total[e] = term

                @pl.when(seen[e] > 0)
                def _():
                    total[e] += term

                seen[e] = 1

        return carry

    lax.fori_loop(0, slots, visit, 0)
    for i in range(len(wanted)):

        def expert(j, carry, i=i):
            e = i * per + j

            @pl.when(seen[e] > 0)
            def _():
                rounded[e] = total[e].astype(BF16)

            @pl.when(seen[e] == 0)
            def _():
                rounded[e] = jnp.zeros(rounded.shape[1:], BF16)

            copy(rounded.at[e], sums[i].at[j], sum_sems.at[e]).start()
            return carry

        lax.fori_loop(0, per, expert, 0)
    for s in range(slots):
        copy(result.at[s], result.at[s], out_sems.at[s]).wait()
    for i in range(len(wanted)):
        for j in range(per):
            copy(rounded.at[0], sums[i].at[j], sum_sems.at[i * per + j]).wait()


def taps(place, slots_in, banks, wanted):
    columns, chans = slots_in.shape[0], slots_in.shape[-1]
    slots = CAP * columns
    per, taps_n = banks[0].shape[:2]
    size = min(bank.shape[0] for bank in banks)
    shape = (per, chans, taps_n * chans)
    found = (len(wanted) * per,) + shape[1:]
    out = pl.pallas_call(
        functools.partial(taps_kernel, size, per, wanted, len(banks)),
        out_shape=[jax.ShapeDtypeStruct((columns, CAP, BACK, BS, chans), BF16)]
        + [jax.ShapeDtypeStruct(shape, BF16)] * len(wanted),
        in_specs=[whole(pltpu.SMEM)] + [whole(pltpu.HBM)] * (len(banks) + 1),
        out_specs=[whole(pltpu.HBM)] * (len(wanted) + 1),
        scratch_shapes=[
            pltpu.VMEM((slots,) + banks[0].shape[1:], BF16),
            pltpu.VMEM((slots, LINES, BS, chans), BF16),
            pltpu.VMEM((slots, BACK, BS, chans), BF16),
            pltpu.VMEM((EDGE * SPAN, chans), F32),
            pltpu.VMEM((EDGE * SPAN, chans), F32),
            pltpu.VMEM((3, (BS + 4) * BS, chans), BF16),
            pltpu.VMEM((TAIL + 8, chans), F32),
            pltpu.VMEM((TAIL + 8, chans), F32),
            pltpu.VMEM(found, F32),
            pltpu.VMEM(found, BF16),
            pltpu.SMEM((found[0],), jnp.int32),
        ]
        + [pltpu.SemaphoreType.DMA((slots,))] * 3
        + [pltpu.SemaphoreType.DMA((found[0],))],
        compiler_params=params(GRANT),
        cost_estimate=pl.CostEstimate(
            flops=200_000_000 * slots, bytes_accessed=800_000 * slots, transcendentals=0
        ),
        name="taps",
    )(place, slots_in, *banks)
    return out[0], out[1:]


def grads_kernel(piece, per, terms, extras, place, slots_in, *refs):
    added, refs = refs[:terms], refs[terms + extras :]
    (out, _, stage, extra, total, wide, result, seen, load_sems, extra_sems,
     out_sems) = refs
    slots = CAP * slots_in.shape[0]
    chans = wide.shape[1]
    for s in range(slots):

        @pl.when(lax.div(place[s // CAP, s % CAP], per) == piece)
        def _():
            copy(slots_in.at[s // CAP, s % CAP], stage.at[s], load_sems.at[s]).start()

    for j in range(per):
        seen[j] = 0
        for i, term in enumerate(added):
            copy(term.at[j], extra.at[i, j], extra_sems.at[i * per + j]).start()

    def visit(s, carry):
        index = place[lax.div(s, CAP), lax.rem(s, CAP)]

        @pl.when(lax.div(index, per) == piece)
        def _():
            j = lax.rem(index, per)
            copy(stage.at[s], stage.at[s], load_sems.at[s]).wait()
            data = stage.at[s]
            term = lax.dot_general(
                data[0:BS].reshape(CELLS, chans),
                nine_taps(shifted_windows(data, wide)),
                (((0,), (0,)), ((), ())),
                preferred_element_type=F32,
            )

            @pl.when(seen[j] == 0)
            def _():
                total[j] = term

            @pl.when(seen[j] > 0)
            def _():
                total[j] += term

            seen[j] = 1

        return carry

    lax.fori_loop(0, slots, visit, 0)

    def expert(j, carry):
        for i in range(terms):
            copy(extra.at[i, j], extra.at[i, j], extra_sems.at[i * per + j]).wait()

        @pl.when(seen[j] > 0)
        def _():
            value = total[j]
            for i in range(terms):
                value = value + extra[i, j].astype(F32)
            result[j] = value.astype(result.dtype)

        @pl.when(seen[j] == 0)
        def _():
            value = jnp.zeros(result.shape[1:], F32)
            for i in range(terms):
                value = value + extra[i, j].astype(F32)
            result[j] = value.astype(result.dtype)

        copy(result.at[j], out.at[j], out_sems.at[j]).start()
        return carry

    lax.fori_loop(0, per, expert, 0)
    for j in range(per):
        copy(result.at[j], out.at[j], out_sems.at[j]).wait()


def grads(place, slots_in, piece, bank_shape, added, after, dtype):
    per, taps_n, chans, outs = bank_shape
    slots = CAP * slots_in.shape[0]
    terms = max(len(added), 1)
    shape = (per, outs, taps_n * chans)
    inputs = [place, slots_in] + list(added) + list(after)
    return pl.pallas_call(
        functools.partial(grads_kernel, piece, per, len(added), len(after)),
        out_shape=[jax.ShapeDtypeStruct(shape, dtype), TOKEN],
        in_specs=[whole(pltpu.SMEM)] + [whole(pltpu.HBM)] * (len(inputs) - 1),
        out_specs=[whole(pltpu.HBM)] * 2,
        scratch_shapes=[
            pltpu.VMEM((slots, LINES, BS, chans), BF16),
            pltpu.VMEM((terms, per if added else 1) + shape[1:], BF16),
            pltpu.VMEM(shape, F32),
            pltpu.VMEM((EDGE * SPAN, chans), F32),
            pltpu.VMEM(shape, dtype),
            pltpu.SMEM((per,), jnp.int32),
            pltpu.SemaphoreType.DMA((slots,)),
            pltpu.SemaphoreType.DMA((terms * per,)),
            pltpu.SemaphoreType.DMA((per,)),
        ],
        compiler_params=params(GRANT),
        cost_estimate=pl.CostEstimate(
            flops=300_000_000, bytes_accessed=6_000_000, transcendentals=0
        ),
        name="grads",
    )(*inputs)


def bank_kernel(count, *refs):
    terms, refs = refs[:count], refs[count:]
    out = refs[0]
    stages, refs = refs[2 : count + 2], refs[count + 2 :]
    result, load_sems, out_sems = refs
    per, taps_n, chans, outs = out.shape
    for j in range(per):
        for i, (term, stage) in enumerate(zip(terms, stages)):
            copy(term.at[j], stage.at[j], load_sems.at[i * per + j]).start()

    def expert(j, carry):
        for i, stage in enumerate(stages):
            copy(stage.at[j], stage.at[j], load_sems.at[i * per + j]).wait()
        for t in range(taps_n):
            columns = slice(t * chans, (t + 1) * chans)
            value = stages[0][j, :, columns].astype(F32)
            for stage in stages[1:]:
                value = value + stage[j, :, columns].astype(F32)
            result[j, t] = value.T
        copy(result.at[j], out.at[j], out_sems.at[j]).start()
        return carry

    lax.fori_loop(0, per, expert, 0)
    for j in range(per):
        copy(result.at[j], out.at[j], out_sems.at[j]).wait()


def bank_of(terms, bank_shape):
    per = bank_shape[0]
    return pl.pallas_call(
        functools.partial(bank_kernel, len(terms)),
        out_shape=[jax.ShapeDtypeStruct(bank_shape, F32), TOKEN],
        in_specs=[whole(pltpu.HBM)] * len(terms),
        out_specs=[whole(pltpu.HBM)] * 2,
        scratch_shapes=[pltpu.VMEM(term.shape, term.dtype) for term in terms]
        + [
            pltpu.VMEM(bank_shape, F32),
            pltpu.SemaphoreType.DMA((len(terms) * per,)),
            pltpu.SemaphoreType.DMA((per,)),
        ],
        compiler_params=params(24),
        cost_estimate=pl.CostEstimate(flops=0, bytes_accessed=12_000_000, transcendentals=0),
        name="bank",
    )(*terms)


def canvas_kernel(per, columns, shape, extras, experts, owner, source, *refs):
    refs = refs[extras:]
    canvas, north, south, west, east, blocks, numbers, counts = refs
    height, width, chans = shape
    stride = width + 2 * GAP
    plan_slots(experts, owner, blocks, numbers, counts, per, columns)

    def clear(r, carry):
        start = pl.multiple_of(r * stride, 8)
        canvas[pl.ds(start, stride), :] = jnp.zeros((stride, chans), F32)
        return carry

    lax.fori_loop(0, height + 2, clear, 0)

    def visit(s, carry):
        data = source.at[lax.div(s, CAP), lax.rem(s, CAP)]
        held = blocks[s]

        @pl.when(held >= 0)
        def _():
            top, left = corner(held, experts.shape[1])
            for u in range(EDGE):
                place = pl.ds(pl.multiple_of((top + u) * stride + GAP + left, 8), BS)
                canvas[place, :] = canvas[place, :] + data[BS + u].astype(F32)
            tail = data[BS + EDGE : BACK].reshape(TAIL, chans).astype(F32)
            start = top * stride + left
            place = pl.ds(start + GAP - 1, EDGE, stride=stride)
            canvas[place, :] = canvas[place, :] + tail[0:EDGE]
            place = pl.ds(start + GAP + BS, EDGE, stride=stride)
            canvas[place, :] = canvas[place, :] + tail[EDGE : 2 * EDGE]

        return carry

    lax.fori_loop(0, columns * CAP, visit, 0)
    north[...] = canvas[0:stride, :].astype(BF16)
    south[...] = canvas[(height + 1) * stride : (height + 2) * stride, :].astype(BF16)
    west[...] = canvas[pl.ds(stride + GAP - 1, height, stride=stride), :]
    east[...] = canvas[pl.ds(stride + GAP + width, height, stride=stride), :]


def canvas_of(experts, owner, source, after, shape, per):
    height, width, chans = shape
    columns = source.shape[0]
    stride = width + 2 * GAP
    return pl.pallas_call(
        functools.partial(canvas_kernel, per, columns, shape, len(after)),
        out_shape=(
            jax.ShapeDtypeStruct(((height + SPARE) * stride, chans), F32),
            jax.ShapeDtypeStruct((stride, chans), BF16),
            jax.ShapeDtypeStruct((stride, chans), BF16),
            jax.ShapeDtypeStruct((height, chans), F32),
            jax.ShapeDtypeStruct((height, chans), F32),
        ),
        in_specs=[whole(pltpu.SMEM)] * 2
        + [whole()]
        + [whole(pltpu.HBM)] * len(after),
        out_specs=(whole(),) * 5,
        scratch_shapes=tables(columns),
        compiler_params=params(16),
        cost_estimate=pl.CostEstimate(flops=0, bytes_accessed=6_000_000, transcendentals=0),
        name="canvas",
    )(experts, owner, source, *after)


def outputs_kernel(per, columns, experts, owner, source, out, _, blocks, numbers, counts, sems):
    plan_slots(experts, owner, blocks, numbers, counts, per, columns)
    for wait in (False, True):
        for s in range(columns * CAP):
            held = blocks[s]

            @pl.when(held >= 0)
            def _():
                top, left = corner(held, experts.shape[1])
                target = out.at[pl.ds(top, BS), pl.ds(left, BS), :]
                move = copy(source.at[s // CAP, s % CAP, pl.ds(0, BS)], target, sems.at[s])
                if wait:
                    move.wait()
                else:
                    move.start()


def outputs_of(experts, owner, source, shape, per):
    columns = source.shape[0]
    return pl.pallas_call(
        functools.partial(outputs_kernel, per, columns),
        out_shape=[jax.ShapeDtypeStruct(shape, BF16), TOKEN],
        in_specs=[whole(pltpu.SMEM)] * 2 + [whole()],
        out_specs=[whole(pltpu.HBM)] * 2,
        scratch_shapes=tables(columns) + [pltpu.SemaphoreType.DMA((columns * CAP,))],
        compiler_params=params(16),
        cost_estimate=pl.CostEstimate(flops=0, bytes_accessed=3_000_000, transcendentals=0),
        name="outputs",
    )(experts, owner, source)


def finish_kernel(canvas, north, south, west, east, _, out):
    height, width, chans = out.shape
    stride = width + 2 * GAP
    column = lax.broadcasted_iota(jnp.int32, (BS, chans), 0)
    for r in range(height):
        start = (r + 1) * stride + GAP
        line = canvas[start : start + width, :]
        if r == 0:
            line = line + north[GAP : GAP + width, :].astype(F32)
        if r == height - 1:
            line = line + south[GAP : GAP + width, :].astype(F32)
        first = line[:BS] + jnp.where(column == 0, west[r : r + 1, :].astype(F32), 0.0)
        last = line[width - BS :] + jnp.where(
            column == BS - 1, east[r : r + 1, :].astype(F32), 0.0
        )
        out[r] = jnp.concatenate([first, line[BS : width - BS], last], axis=0).astype(BF16)


def finish(canvas, north, south, west, east, after, shape):
    return pl.pallas_call(
        finish_kernel,
        out_shape=jax.ShapeDtypeStruct(shape, BF16),
        in_specs=[whole()] * 5 + [whole(pltpu.HBM)],
        out_specs=whole(),
        compiler_params=params(16),
        cost_estimate=pl.CostEstimate(flops=0, bytes_accessed=4_000_000, transcendentals=0),
        name="finish",
    )(canvas, north, south, west, east, after)


def across(array, axis, shift, wrap):
    count = lax.axis_size(axis)
    pairs = [(i, i + shift) for i in range(count)]
    if wrap:
        pairs = [(i, j % count) for i, j in pairs]
    else:
        pairs = [(i, j) for i, j in pairs if 0 <= j < count]
    return lax.ppermute(array, axis, pairs)


def to_other_core(array):
    return lax.ppermute(array, "lat", [(i, i ^ 1) for i in range(lax.axis_size("lat"))])


def to_chip(array, shift):
    count = lax.axis_size("lat")
    return lax.ppermute(array, "lat", [(i, (i + 2 * shift) % count) for i in range(count)])


def exchange(array):
    return lax.all_to_all(array, "lon", split_axis=0, concat_axis=0, tiled=True)


def tied(arrays, others):
    return lax.optimization_barrier((arrays, others))[0]


def places_of(slots, chips, per):
    lat_index = lax.axis_index("lat")
    line, row = OWN + NUMBER // BS, NUMBER % BS
    numbers = slots[:, :, line, row, 0].astype(jnp.int32)
    owner_lat = numbers // per
    chip_step = (owner_lat // 2 - lat_index // 2 + chips) % chips
    core_step = (owner_lat % 2 - lat_index % 2 + 2) % 2
    return (2 * chip_step + core_step) * per + numbers % per


def local(fields, cotangent, kernel_bank, block_expert, owner):
    columns = lax.axis_size("lon")
    chips = lax.axis_size("lat") // 2
    per = kernel_bank.shape[0]
    shape = kernel_bank.shape

    north = across(fields[-1:], "lat", 1, False)
    south = across(fields[:1], "lat", -1, False)
    filled, _ = dispatch_own(block_expert, owner, fields, cotangent, per, columns)
    first, last = rims_of(
        north, south, fields[:, 0].astype(F32), fields[:, -1].astype(F32)
    )
    west = across(last, "lon", 1, True)
    east = across(first, "lon", -1, True)
    filled = dispatch_rings(
        block_expert, owner, fields, north, south, west, east, filled, per
    )
    arrived = exchange(filled)
    place = places_of(arrived, chips, per)
    slots = (place, arrived)

    banks = [kernel_bank, to_other_core(tied(kernel_bank, (west, east)))]
    for k in range(1, chips):
        distant = to_chip(tied(kernel_bank, (first, last)), -k)
        banks += [distant, to_other_core(distant)]

    results, beside = taps(
        place, arrived, banks, tuple(2 * k + 1 for k in range(1, chips))
    )
    results = exchange(results)
    beside = [to_other_core(part) for part in beside]
    chip_parts, tokens = [], []
    for k in range(1, chips):
        part, token = grads(*slots, 2 * k, shape, [beside[k - 1]], tokens, BF16)
        chip_parts.append(to_chip(part, k))
        tokens = [token]
    core_part, core_token = grads(*slots, 1, shape, [], tokens, BF16)
    own_part, own_token = grads(*slots, 0, shape, [], tokens, F32)
    terms = [own_part, to_other_core(core_part)] + chip_parts

    canvas, top, bottom, left, right = canvas_of(
        block_expert, owner, results, [core_token, own_token], fields.shape, per
    )
    above = across(bottom, "lat", 1, False)
    below = across(top, "lat", -1, False)
    outputs, token = outputs_of(block_expert, owner, results, fields.shape, per)
    left, right = corners_of(above, below, left, right, token)
    from_west = across(right, "lon", 1, True)
    from_east = across(left, "lon", -1, True)
    grad_bank, token = bank_of(terms, shape)
    grad_fields = finish(canvas, above, below, from_west, from_east, token, fields.shape)
    return (outputs, grad_fields, grad_bank)


def solution(mesh):
    return jax.shard_map(
        local,
        mesh=mesh,
        in_specs=(
            P("lat", "lon", None),
            P("lat", "lon", None),
            P(("lat", "lon"), None, None, None),
            P("lat", "lon"),
            P(),
        ),
        out_specs=(
            P("lat", "lon", None),
            P("lat", "lon", None),
            P(("lat", "lon"), None, None, None),
        ),
        check_vma=False,
    )
```

```python
import functools

import jax
import jax.numpy as jnp
from jax import lax
from jax.experimental import pallas as pl
from jax.experimental.pallas import tpu as pltpu
from jax.sharding import PartitionSpec as P

BS = 16
CAP = 2
EDGE = BS + 2
CELLS = BS * BS
MAIN = EDGE * BS
TAIL = 48
OWN = 2 * BS
RING = 5
LINES = OWN + RING
NUMBER = 4 * BS + 4
WINDOW = EDGE + TAIL // BS
BACK = BS + WINDOW
SPARE = 8
GAP = 8
SPAN = 2 * BS
GRANT = 59
F32 = jnp.float32
BF16 = jnp.bfloat16


def params(mib):
    return pltpu.CompilerParams(vmem_limit_bytes=mib * 1024 * 1024)


TOKEN = jax.ShapeDtypeStruct((8, 128), jnp.float32)


def whole(memory=pltpu.VMEM):
    return pl.BlockSpec(memory_space=memory)


def copy(source, target, sem):
    return pltpu.make_async_copy(source, target, sem)


def corner(block, lon_blocks):
    top = lax.div(block, lon_blocks) * BS
    return top, pl.multiple_of(lax.rem(block, lon_blocks) * BS, BS)


def tables(columns):
    return [
        pltpu.SMEM((columns * CAP,), jnp.int32),
        pltpu.SMEM((columns * CAP,), jnp.int32),
        pltpu.SMEM((columns,), jnp.int32),
    ]


def plan_slots(experts, owner, blocks, numbers, counts, per, columns):
    lat_blocks, lon_blocks = experts.shape

    def clear_slot(s, carry):
        blocks[s] = -1
        numbers[s] = 0
        return carry

    def clear_count(s, carry):
        counts[s] = 0
        return carry

    lax.fori_loop(0, columns * CAP, clear_slot, 0)
    lax.fori_loop(0, columns, clear_count, 0)

    def place(b, carry):
        stored = owner[experts[lax.div(b, lon_blocks), lax.rem(b, lon_blocks)]]
        group = lax.div(stored, per)
        column = lax.rem(group, columns)
        rank = counts[column]
        counts[column] = rank + 1
        slot = column * CAP + rank
        blocks[slot] = b
        numbers[slot] = lax.div(group, columns) * per + lax.rem(stored, per)
        return carry

    lax.fori_loop(0, lat_blocks * lon_blocks, place, 0)


def own_kernel(per, columns, experts, owner, fields, cot, *refs):
    out, _, grid, cells, blank, blocks, numbers, counts, load_sems, sems = refs
    height, width, chans = fields.shape
    sources = (cells, grid)
    loads = [copy(cot, cells, load_sems.at[0]), copy(fields, grid, load_sems.at[1])]
    for load in loads:
        load.start()
    plan_slots(experts, owner, blocks, numbers, counts, per, columns)
    blank[...] = jnp.zeros(blank.shape, BF16)
    for part, source in enumerate(sources):
        loads[part].wait()
        for column in range(columns):
            for r in range(CAP):
                s = column * CAP + r
                held = blocks[s]
                top, left = corner(jnp.maximum(held, 0), experts.shape[1])
                target = out.at[column, r, pl.ds(part * BS, BS)]

                @pl.when(held >= 0)
                def _():
                    copy(
                        source.at[pl.ds(top, BS), pl.ds(left, BS), :], target, sems.at[part, s]
                    ).start()

                @pl.when(held < 0)
                def _():
                    copy(blank, target, sems.at[part, s]).start()

    for part in range(2):
        for s in range(columns * CAP):
            copy(blank, out.at[0, 0, pl.ds(0, BS)], sems.at[part, s]).wait()


def dispatch_own(experts, owner, fields, cot, per, columns):
    chans = cot.shape[2]
    out = pl.pallas_call(
        functools.partial(own_kernel, per, columns),
        out_shape=[
            jax.ShapeDtypeStruct((columns, CAP, LINES, BS, chans), BF16),
            TOKEN,
        ],
        in_specs=[whole(pltpu.SMEM)] * 2 + [whole(pltpu.HBM)] * 2,
        out_specs=[whole(pltpu.HBM)] * 2,
        scratch_shapes=[
            pltpu.VMEM(fields.shape, BF16),
            pltpu.VMEM(cot.shape, BF16),
            pltpu.VMEM((BS, BS, chans), BF16),
        ]
        + tables(columns)
        + [pltpu.SemaphoreType.DMA((2,)), pltpu.SemaphoreType.DMA((2, columns * CAP))],
        compiler_params=params(GRANT),
        cost_estimate=pl.CostEstimate(flops=0, bytes_accessed=6_000_000, transcendentals=0),
        name="dispatch_own",
    )(experts, owner, fields, cot)
    return out


def rims_kernel(north, south, first, last, first_out, last_out):
    width = north.shape[1]
    for inner, out, left, column in (
        (first, first_out, 0, 0),
        (last, last_out, width - BS, BS - 1),
    ):
        above = north[0, left : left + BS, :].astype(F32)
        below = south[0, left : left + BS, :].astype(F32)
        out[...] = jnp.concatenate(
            [above[column : column + 1], inner[...], below[column : column + 1]], axis=0
        ).astype(BF16)


def rims_of(north, south, first, last):
    height, chans = first.shape
    return pl.pallas_call(
        rims_kernel,
        out_shape=[jax.ShapeDtypeStruct((height + 2, chans), BF16)] * 2,
        in_specs=[whole()] * 4,
        out_specs=[whole()] * 2,
        compiler_params=params(4),
        name="rims",
    )(north, south, first, last)


def corners_kernel(above, below, left, right, _, left_out, right_out):
    height = left.shape[0]
    row = lax.broadcasted_iota(jnp.int32, left.shape, 0)
    stride = above.shape[0]
    for line, out, start, column in (
        (left, left_out, 0, GAP - 1),
        (right, right_out, stride - BS, BS - GAP),
    ):
        top = above[start : start + BS, :].astype(F32)[column : column + 1]
        bottom = below[start : start + BS, :].astype(F32)[column : column + 1]
        out[...] = (
            line[...]
            + jnp.where(row == 0, top, 0.0)
            + jnp.where(row == height - 1, bottom, 0.0)
        ).astype(BF16)


def corners_of(above, below, left, right, after):
    return pl.pallas_call(
        corners_kernel,
        out_shape=[jax.ShapeDtypeStruct(left.shape, BF16)] * 2,
        in_specs=[whole()] * 4 + [whole(pltpu.HBM)],
        out_specs=[whole()] * 2,
        compiler_params=params(4),
        name="corners",
    )(above, below, left, right, after)


def ring_kernel(
    per, columns, experts, owner, fields, north, south, west, east, _, out, rows, wide, rings,
    blocks, numbers, counts, load_sem, sems,
):
    height, width, chans = fields.shape
    stride = width + 2 * GAP
    load = copy(fields, rows.at[pl.ds(1, height)], load_sem)
    load.start()
    plan_slots(experts, owner, blocks, numbers, counts, per, columns)
    rows[0] = north[0]
    rows[height + 1] = south[0]
    load.wait()

    def widen(r, carry):
        start = pl.multiple_of(r * stride + GAP, 8)
        wide[pl.ds(start, width), :] = rows[r].astype(F32)
        return carry

    lax.fori_loop(0, height + 2, widen, 0)
    wide[pl.ds(GAP - 1, height + 2, stride=stride), :] = west[...].astype(F32)
    wide[pl.ds(GAP + width, height + 2, stride=stride), :] = east[...].astype(F32)
    for s in range(columns * CAP):
        top, left = corner(jnp.maximum(blocks[s], 0), experts.shape[1])
        start = pl.multiple_of(top * stride + left, 8)
        upper = wide[pl.ds(start, BS + 2 * GAP), :]
        start = pl.multiple_of(start + (EDGE - 1) * stride, 8)
        lower = wide[pl.ds(start, BS + 2 * GAP), :]
        start = (top + 1) * stride + left
        ring = jnp.concatenate(
            [
                upper[GAP - 1 : GAP + BS + 1],
                lower[GAP - 1 : GAP + BS + 1],
                wide[pl.ds(start + GAP - 1, BS, stride=stride), :],
                wide[pl.ds(start + GAP + BS, BS, stride=stride), :],
                jnp.full((RING * BS - NUMBER, chans), numbers[s].astype(F32), F32),
            ],
            axis=0,
        )
        rings[s] = ring.astype(BF16).reshape(RING, BS, chans)
        target = out.at[s // CAP, s % CAP, pl.ds(OWN, RING)]
        copy(rings.at[s], target, sems.at[s]).start()
    for s in range(columns * CAP):
        target = out.at[s // CAP, s % CAP, pl.ds(OWN, RING)]
        copy(rings.at[s], target, sems.at[s]).wait()


def dispatch_rings(experts, owner, fields, north, south, west, east, filled, per):
    height, width, chans = fields.shape
    columns = filled.shape[0]
    slots = columns * CAP
    return pl.pallas_call(
        functools.partial(ring_kernel, per, columns),
        out_shape=jax.ShapeDtypeStruct(filled.shape, BF16),
        in_specs=[whole(pltpu.SMEM)] * 2
        + [whole(pltpu.HBM)]
        + [whole()] * 4
        + [whole(pltpu.HBM)],
        out_specs=whole(pltpu.HBM),
        input_output_aliases={7: 0},
        scratch_shapes=[
            pltpu.VMEM((height + 2, width, chans), BF16),
            pltpu.VMEM(((height + SPARE) * (width + 2 * GAP), chans), F32),
            pltpu.VMEM((slots, RING, BS, chans), BF16),
        ]
        + tables(columns)
        + [pltpu.SemaphoreType.DMA, pltpu.SemaphoreType.DMA((slots,))],
        compiler_params=params(GRANT),
        cost_estimate=pl.CostEstimate(flops=0, bytes_accessed=3_000_000, transcendentals=0),
        name="dispatch_rings",
    )(experts, owner, fields, north, south, west, east, filled)


def shifted_windows(data, wide):
    chans = wide.shape[1]
    ring = data[OWN:LINES].reshape(RING * BS, chans).astype(F32)
    bottom = SPAN * (EDGE - 1)
    wide[7 : 7 + EDGE, :] = ring[0:EDGE]
    wide[bottom + 7 : bottom + 7 + EDGE, :] = ring[EDGE : 2 * EDGE]
    wide[pl.ds(SPAN + 7, BS, stride=SPAN), :] = ring[2 * EDGE : 2 * EDGE + BS]
    wide[pl.ds(SPAN + 8 + BS, BS, stride=SPAN), :] = ring[2 * EDGE + BS : NUMBER]
    for x in range(BS):
        start = SPAN * (x + 1) + 8
        wide[start : start + BS, :] = data[BS + x].astype(F32)
    first = [wide[SPAN * u + 7 : SPAN * u + 7 + BS, :] for u in range(EDGE)]
    third = [wide[SPAN * u + 9 : SPAN * u + 9 + BS, :] for u in range(EDGE)]
    return (
        jnp.concatenate(first, axis=0).astype(BF16),
        jnp.concatenate(
            [
                wide[8 : 8 + BS, :].astype(BF16),
                data[BS:OWN].reshape(CELLS, chans),
                wide[bottom + 8 : bottom + 8 + BS, :].astype(BF16),
            ],
            axis=0,
        ),
        jnp.concatenate(third, axis=0).astype(BF16),
    )


def nine_taps(windows):
    return jnp.concatenate(
        [w[BS * a : BS * a + CELLS] for a in range(3) for w in windows], axis=1
    )


def load_bank(index, banks, target, sem, size):
    piece = lax.div(index, size)
    row = lax.rem(index, size)
    p = 0
    for bank in banks:
        for start in range(0, bank.shape[0], size):

            @pl.when(piece == p)
            def _():
                copy(bank.at[start + row], target, sem).start()

            p += 1


def taps_kernel(size, per, wanted, pieces, place, slots_in, *refs):
    banks, refs = refs[:pieces], refs[pieces:]
    out, sums, refs = refs[0], refs[1 : len(wanted) + 1], refs[len(wanted) + 1 :]
    (held, stage, result, wide, cots, lines, before, after, total, rounded, seen, bank_sems,
     load_sems, out_sems, sum_sems) = refs
    chans = cots.shape[1]
    slots = CAP * slots_in.shape[0]
    for s in range(slots):
        copy(slots_in.at[s // CAP, s % CAP], stage.at[s], load_sems.at[s]).start()
        load_bank(place[s // CAP, s % CAP], banks, held.at[s], bank_sems.at[s], size)
    for e in range(len(wanted) * per):
        seen[e] = 0
    cots[...] = jnp.zeros(cots.shape, F32)
    lines[...] = jnp.zeros(lines.shape, BF16)
    before[...] = jnp.zeros(before.shape, F32)
    after[...] = jnp.zeros(after.shape, F32)

    def visit(s, carry):
        copy(stage.at[s], stage.at[s], load_sems.at[s]).wait()
        copy(held.at[s], held.at[s], bank_sems.at[s]).wait()
        data = stage.at[s]
        bank = held.at[s]
        for x in range(BS):
            cots[SPAN * x + 8 : SPAN * x + 8 + BS, :] = data[x].astype(F32)
            lines[1, BS * (x + 2) : BS * (x + 3), :] = data[x]
        for x in range(BS):
            lines[0, BS * (x + 2) : BS * (x + 3), :] = cots[
                SPAN * x + 9 : SPAN * x + 9 + BS, :
            ].astype(BF16)
            lines[2, BS * (x + 2) : BS * (x + 3), :] = cots[
                SPAN * x + 7 : SPAN * x + 7 + BS, :
            ].astype(BF16)
        before[2 : 2 + BS, :] = cots[pl.ds(8, BS, stride=SPAN), :]
        after[EDGE + 2 : EDGE + 2 + BS, :] = cots[pl.ds(8 + BS - 1, BS, stride=SPAN), :]
        sides = []
        for a in range(3):
            for b in range(3):
                if b == 0:
                    tail = before[2 - a : 2 - a + TAIL, :].astype(BF16)
                elif b == 2:
                    tail = after[2 - a : 2 - a + TAIL, :].astype(BF16)
                else:
                    tail = jnp.zeros((TAIL, chans), BF16)
                main = lines[b, (2 - a) * BS : (2 - a) * BS + MAIN, :]
                sides.append(jnp.concatenate([main, tail], axis=0))
        spread = lax.dot_general(
            jnp.concatenate(sides, axis=1),
            jnp.concatenate([bank[t] for t in range(9)], axis=1),
            (((1,), (1,)), ((), ())),
            preferred_element_type=F32,
        )
        result[s, BS:] = spread.astype(BF16).reshape(WINDOW, BS, chans)
        windows = nine_taps(shifted_windows(data, wide))
        output = jnp.dot(
            windows,
            bank[...].reshape(9 * chans, chans),
            preferred_element_type=F32,
        )
        result[s, 0:BS] = output.astype(BF16).reshape(BS, BS, chans)
        target = out.at[lax.div(s, CAP), lax.rem(s, CAP)]
        copy(result.at[s], target, out_sems.at[s]).start()
        index = place[lax.div(s, CAP), lax.rem(s, CAP)]
        piece = lax.div(index, per)
        for i, p in enumerate(wanted):

            @pl.when(piece == p)
            def _():
                e = i * per + lax.rem(index, per)
                term = lax.dot_general(
                    data[0:BS].reshape(CELLS, chans),
                    windows,
                    (((0,), (0,)), ((), ())),
                    preferred_element_type=F32,
                )

                @pl.when(seen[e] == 0)
                def _():
                    total[e] = term

                @pl.when(seen[e] > 0)
                def _():
                    total[e] += term

                seen[e] = 1

        return carry

    lax.fori_loop(0, slots, visit, 0)
    for i in range(len(wanted)):

        def expert(j, carry, i=i):
            e = i * per + j

            @pl.when(seen[e] > 0)
            def _():
                rounded[e] = total[e].astype(BF16)

            @pl.when(seen[e] == 0)
            def _():
                rounded[e] = jnp.zeros(rounded.shape[1:], BF16)

            copy(rounded.at[e], sums[i].at[j], sum_sems.at[e]).start()
            return carry

        lax.fori_loop(0, per, expert, 0)
    for s in range(slots):
        copy(result.at[s], result.at[s], out_sems.at[s]).wait()
    for i in range(len(wanted)):
        for j in range(per):
            copy(rounded.at[0], sums[i].at[j], sum_sems.at[i * per + j]).wait()


def taps(place, slots_in, banks, wanted):
    columns, chans = slots_in.shape[0], slots_in.shape[-1]
    slots = CAP * columns
    per, taps_n = banks[0].shape[:2]
    size = min(bank.shape[0] for bank in banks)
    shape = (per, chans, taps_n * chans)
    found = (len(wanted) * per,) + shape[1:]
    out = pl.pallas_call(
        functools.partial(taps_kernel, size, per, wanted, len(banks)),
        out_shape=[jax.ShapeDtypeStruct((columns, CAP, BACK, BS, chans), BF16)]
        + [jax.ShapeDtypeStruct(shape, BF16)] * len(wanted),
        in_specs=[whole(pltpu.SMEM)] + [whole(pltpu.HBM)] * (len(banks) + 1),
        out_specs=[whole(pltpu.HBM)] * (len(wanted) + 1),
        scratch_shapes=[
            pltpu.VMEM((slots,) + banks[0].shape[1:], BF16),
            pltpu.VMEM((slots, LINES, BS, chans), BF16),
            pltpu.VMEM((slots, BACK, BS, chans), BF16),
            pltpu.VMEM((EDGE * SPAN, chans), F32),
            pltpu.VMEM((EDGE * SPAN, chans), F32),
            pltpu.VMEM((3, (BS + 4) * BS, chans), BF16),
            pltpu.VMEM((TAIL + 8, chans), F32),
            pltpu.VMEM((TAIL + 8, chans), F32),
            pltpu.VMEM(found, F32),
            pltpu.VMEM(found, BF16),
            pltpu.SMEM((found[0],), jnp.int32),
        ]
        + [pltpu.SemaphoreType.DMA((slots,))] * 3
        + [pltpu.SemaphoreType.DMA((found[0],))],
        compiler_params=params(GRANT),
        cost_estimate=pl.CostEstimate(
            flops=200_000_000 * slots, bytes_accessed=800_000 * slots, transcendentals=0
        ),
        name="taps",
    )(place, slots_in, *banks)
    return out[0], out[1:]


def grads_kernel(piece, per, terms, extras, place, slots_in, *refs):
    added, refs = refs[:terms], refs[terms + extras :]
    (out, _, stage, extra, total, wide, result, seen, load_sems, extra_sems,
     out_sems) = refs
    slots = CAP * slots_in.shape[0]
    chans = wide.shape[1]
    for s in range(slots):

        @pl.when(lax.div(place[s // CAP, s % CAP], per) == piece)
        def _():
            copy(slots_in.at[s // CAP, s % CAP], stage.at[s], load_sems.at[s]).start()

    for j in range(per):
        seen[j] = 0
        for i, term in enumerate(added):
            copy(term.at[j], extra.at[i, j], extra_sems.at[i * per + j]).start()

    def visit(s, carry):
        index = place[lax.div(s, CAP), lax.rem(s, CAP)]

        @pl.when(lax.div(index, per) == piece)
        def _():
            j = lax.rem(index, per)
            copy(stage.at[s], stage.at[s], load_sems.at[s]).wait()
            data = stage.at[s]
            term = lax.dot_general(
                data[0:BS].reshape(CELLS, chans),
                nine_taps(shifted_windows(data, wide)),
                (((0,), (0,)), ((), ())),
                preferred_element_type=F32,
            )

            @pl.when(seen[j] == 0)
            def _():
                total[j] = term

            @pl.when(seen[j] > 0)
            def _():
                total[j] += term

            seen[j] = 1

        return carry

    lax.fori_loop(0, slots, visit, 0)

    def expert(j, carry):
        for i in range(terms):
            copy(extra.at[i, j], extra.at[i, j], extra_sems.at[i * per + j]).wait()

        @pl.when(seen[j] > 0)
        def _():
            value = total[j]
            for i in range(terms):
                value = value + extra[i, j].astype(F32)
            result[j] = value.astype(result.dtype)

        @pl.when(seen[j] == 0)
        def _():
            value = jnp.zeros(result.shape[1:], F32)
            for i in range(terms):
                value = value + extra[i, j].astype(F32)
            result[j] = value.astype(result.dtype)

        copy(result.at[j], out.at[j], out_sems.at[j]).start()
        return carry

    lax.fori_loop(0, per, expert, 0)
    for j in range(per):
        copy(result.at[j], out.at[j], out_sems.at[j]).wait()


def grads(place, slots_in, piece, bank_shape, added, after, dtype):
    per, taps_n, chans, outs = bank_shape
    slots = CAP * slots_in.shape[0]
    terms = max(len(added), 1)
    shape = (per, outs, taps_n * chans)
    inputs = [place, slots_in] + list(added) + list(after)
    return pl.pallas_call(
        functools.partial(grads_kernel, piece, per, len(added), len(after)),
        out_shape=[jax.ShapeDtypeStruct(shape, dtype), TOKEN],
        in_specs=[whole(pltpu.SMEM)] + [whole(pltpu.HBM)] * (len(inputs) - 1),
        out_specs=[whole(pltpu.HBM)] * 2,
        scratch_shapes=[
            pltpu.VMEM((slots, LINES, BS, chans), BF16),
            pltpu.VMEM((terms, per if added else 1) + shape[1:], BF16),
            pltpu.VMEM(shape, F32),
            pltpu.VMEM((EDGE * SPAN, chans), F32),
            pltpu.VMEM(shape, dtype),
            pltpu.SMEM((per,), jnp.int32),
            pltpu.SemaphoreType.DMA((slots,)),
            pltpu.SemaphoreType.DMA((terms * per,)),
            pltpu.SemaphoreType.DMA((per,)),
        ],
        compiler_params=params(GRANT),
        cost_estimate=pl.CostEstimate(
            flops=300_000_000, bytes_accessed=6_000_000, transcendentals=0
        ),
        name="grads",
    )(*inputs)


def bank_kernel(count, *refs):
    terms, refs = refs[:count], refs[count:]
    out = refs[0]
    stages, refs = refs[2 : count + 2], refs[count + 2 :]
    result, load_sems, out_sems = refs
    per, taps_n, chans, outs = out.shape
    for j in range(per):
        for i, (term, stage) in enumerate(zip(terms, stages)):
            copy(term.at[j], stage.at[j], load_sems.at[i * per + j]).start()

    def expert(j, carry):
        for i, stage in enumerate(stages):
            copy(stage.at[j], stage.at[j], load_sems.at[i * per + j]).wait()
        for t in range(taps_n):
            columns = slice(t * chans, (t + 1) * chans)
            value = stages[0][j, :, columns].astype(F32)
            for stage in stages[1:]:
                value = value + stage[j, :, columns].astype(F32)
            result[j, t] = value.T
        copy(result.at[j], out.at[j], out_sems.at[j]).start()
        return carry

    lax.fori_loop(0, per, expert, 0)
    for j in range(per):
        copy(result.at[j], out.at[j], out_sems.at[j]).wait()


def bank_of(terms, bank_shape):
    per = bank_shape[0]
    return pl.pallas_call(
        functools.partial(bank_kernel, len(terms)),
        out_shape=[jax.ShapeDtypeStruct(bank_shape, F32), TOKEN],
        in_specs=[whole(pltpu.HBM)] * len(terms),
        out_specs=[whole(pltpu.HBM)] * 2,
        scratch_shapes=[pltpu.VMEM(term.shape, term.dtype) for term in terms]
        + [
            pltpu.VMEM(bank_shape, F32),
            pltpu.SemaphoreType.DMA((len(terms) * per,)),
            pltpu.SemaphoreType.DMA((per,)),
        ],
        compiler_params=params(24),
        cost_estimate=pl.CostEstimate(flops=0, bytes_accessed=12_000_000, transcendentals=0),
        name="bank",
    )(*terms)


def canvas_kernel(per, columns, shape, extras, experts, owner, source, *refs):
    refs = refs[extras:]
    canvas, north, south, west, east, blocks, numbers, counts = refs
    height, width, chans = shape
    stride = width + 2 * GAP
    plan_slots(experts, owner, blocks, numbers, counts, per, columns)

    def clear(r, carry):
        start = pl.multiple_of(r * stride, 8)
        canvas[pl.ds(start, stride), :] = jnp.zeros((stride, chans), F32)
        return carry

    lax.fori_loop(0, height + 2, clear, 0)

    def visit(s, carry):
        data = source.at[lax.div(s, CAP), lax.rem(s, CAP)]
        held = blocks[s]

        @pl.when(held >= 0)
        def _():
            top, left = corner(held, experts.shape[1])
            for u in range(EDGE):
                place = pl.ds(pl.multiple_of((top + u) * stride + GAP + left, 8), BS)
                canvas[place, :] = canvas[place, :] + data[BS + u].astype(F32)
            tail = data[BS + EDGE : BACK].reshape(TAIL, chans).astype(F32)
            start = top * stride + left
            place = pl.ds(start + GAP - 1, EDGE, stride=stride)
            canvas[place, :] = canvas[place, :] + tail[0:EDGE]
            place = pl.ds(start + GAP + BS, EDGE, stride=stride)
            canvas[place, :] = canvas[place, :] + tail[EDGE : 2 * EDGE]

        return carry

    lax.fori_loop(0, columns * CAP, visit, 0)
    north[...] = canvas[0:stride, :].astype(BF16)
    south[...] = canvas[(height + 1) * stride : (height + 2) * stride, :].astype(BF16)
    west[...] = canvas[pl.ds(stride + GAP - 1, height, stride=stride), :]
    east[...] = canvas[pl.ds(stride + GAP + width, height, stride=stride), :]


def canvas_of(experts, owner, source, after, shape, per):
    height, width, chans = shape
    columns = source.shape[0]
    stride = width + 2 * GAP
    return pl.pallas_call(
        functools.partial(canvas_kernel, per, columns, shape, len(after)),
        out_shape=(
            jax.ShapeDtypeStruct(((height + SPARE) * stride, chans), F32),
            jax.ShapeDtypeStruct((stride, chans), BF16),
            jax.ShapeDtypeStruct((stride, chans), BF16),
            jax.ShapeDtypeStruct((height, chans), F32),
            jax.ShapeDtypeStruct((height, chans), F32),
        ),
        in_specs=[whole(pltpu.SMEM)] * 2
        + [whole()]
        + [whole(pltpu.HBM)] * len(after),
        out_specs=(whole(),) * 5,
        scratch_shapes=tables(columns),
        compiler_params=params(16),
        cost_estimate=pl.CostEstimate(flops=0, bytes_accessed=6_000_000, transcendentals=0),
        name="canvas",
    )(experts, owner, source, *after)


def outputs_kernel(per, columns, experts, owner, source, out, _, blocks, numbers, counts, sems):
    plan_slots(experts, owner, blocks, numbers, counts, per, columns)
    for wait in (False, True):
        for s in range(columns * CAP):
            held = blocks[s]

            @pl.when(held >= 0)
            def _():
                top, left = corner(held, experts.shape[1])
                target = out.at[pl.ds(top, BS), pl.ds(left, BS), :]
                move = copy(source.at[s // CAP, s % CAP, pl.ds(0, BS)], target, sems.at[s])
                if wait:
                    move.wait()
                else:
                    move.start()


def outputs_of(experts, owner, source, shape, per):
    columns = source.shape[0]
    return pl.pallas_call(
        functools.partial(outputs_kernel, per, columns),
        out_shape=[jax.ShapeDtypeStruct(shape, BF16), TOKEN],
        in_specs=[whole(pltpu.SMEM)] * 2 + [whole()],
        out_specs=[whole(pltpu.HBM)] * 2,
        scratch_shapes=tables(columns) + [pltpu.SemaphoreType.DMA((columns * CAP,))],
        compiler_params=params(16),
        cost_estimate=pl.CostEstimate(flops=0, bytes_accessed=3_000_000, transcendentals=0),
        name="outputs",
    )(experts, owner, source)


def finish_kernel(canvas, north, south, west, east, _, out):
    height, width, chans = out.shape
    stride = width + 2 * GAP
    column = lax.broadcasted_iota(jnp.int32, (BS, chans), 0)
    for r in range(height):
        start = (r + 1) * stride + GAP
        line = canvas[start : start + width, :]
        if r == 0:
            line = line + north[GAP : GAP + width, :].astype(F32)
        if r == height - 1:
            line = line + south[GAP : GAP + width, :].astype(F32)
        first = line[:BS] + jnp.where(column == 0, west[r : r + 1, :].astype(F32), 0.0)
        last = line[width - BS :] + jnp.where(
            column == BS - 1, east[r : r + 1, :].astype(F32), 0.0
        )
        out[r] = jnp.concatenate([first, line[BS : width - BS], last], axis=0).astype(BF16)


def finish(canvas, north, south, west, east, after, shape):
    return pl.pallas_call(
        finish_kernel,
        out_shape=jax.ShapeDtypeStruct(shape, BF16),
        in_specs=[whole()] * 5 + [whole(pltpu.HBM)],
        out_specs=whole(),
        compiler_params=params(16),
        cost_estimate=pl.CostEstimate(flops=0, bytes_accessed=4_000_000, transcendentals=0),
        name="finish",
    )(canvas, north, south, west, east, after)


def across(array, axis, shift, wrap):
    count = lax.axis_size(axis)
    pairs = [(i, i + shift) for i in range(count)]
    if wrap:
        pairs = [(i, j % count) for i, j in pairs]
    else:
        pairs = [(i, j) for i, j in pairs if 0 <= j < count]
    return lax.ppermute(array, axis, pairs)


def to_other_core(array):
    return lax.ppermute(array, "lat", [(i, i ^ 1) for i in range(lax.axis_size("lat"))])


def to_chip(array, shift):
    count = lax.axis_size("lat")
    return lax.ppermute(array, "lat", [(i, (i + 2 * shift) % count) for i in range(count)])


def exchange(array):
    return lax.all_to_all(array, "lon", split_axis=0, concat_axis=0, tiled=True)


def tied(arrays, others):
    return lax.optimization_barrier((arrays, others))[0]


def places_of(slots, chips, per):
    lat_index = lax.axis_index("lat")
    line, row = OWN + NUMBER // BS, NUMBER % BS
    numbers = slots[:, :, line, row, 0].astype(jnp.int32)
    owner_lat = numbers // per
    chip_step = (owner_lat // 2 - lat_index // 2 + chips) % chips
    core_step = (owner_lat % 2 - lat_index % 2 + 2) % 2
    return (2 * chip_step + core_step) * per + numbers % per


def local(fields, cotangent, kernel_bank, block_expert, owner):
    columns = lax.axis_size("lon")
    chips = lax.axis_size("lat") // 2
    per = kernel_bank.shape[0]
    shape = kernel_bank.shape

    north = across(fields[-1:], "lat", 1, False)
    south = across(fields[:1], "lat", -1, False)
    filled, _ = dispatch_own(block_expert, owner, fields, cotangent, per, columns)
    first, last = rims_of(
        north, south, fields[:, 0].astype(F32), fields[:, -1].astype(F32)
    )
    west = across(last, "lon", 1, True)
    east = across(first, "lon", -1, True)
    filled = dispatch_rings(
        block_expert, owner, fields, north, south, west, east, filled, per
    )
    arrived = exchange(filled)
    place = places_of(arrived, chips, per)
    slots = (place, arrived)

    banks = [kernel_bank, to_other_core(tied(kernel_bank, (west, east)))]
    for k in range(1, chips):
        distant = to_chip(tied(kernel_bank, (first, last)), -k)
        banks += [distant, to_other_core(distant)]

    results, beside = taps(place, arrived, banks, tuple(range(1, 2 * chips, 2)))
    results = exchange(results)
    beside = [to_other_core(part) for part in beside]
    terms, tokens = [], []
    for k in range(1, chips):
        part, token = grads(*slots, 2 * k, shape, [beside[k]], tokens, BF16)
        terms.append(to_chip(part, k))
        tokens = [token]
    own_part, token = grads(*slots, 0, shape, [], tokens, F32)
    terms = [own_part, beside[0]] + terms

    canvas, top, bottom, left, right = canvas_of(
        block_expert, owner, results, [token], fields.shape, per
    )
    above = across(bottom, "lat", 1, False)
    below = across(top, "lat", -1, False)
    grad_bank, token = bank_of(terms, shape)
    left, right = corners_of(above, below, left, right, token)
    from_west = across(right, "lon", 1, True)
    from_east = across(left, "lon", -1, True)
    outputs, token = outputs_of(block_expert, owner, results, fields.shape, per)
    grad_fields = finish(canvas, above, below, from_west, from_east, token, fields.shape)
    return (outputs, grad_fields, grad_bank)


def solution(mesh):
    return jax.shard_map(
        local,
        mesh=mesh,
        in_specs=(
            P("lat", "lon", None),
            P("lat", "lon", None),
            P(("lat", "lon"), None, None, None),
            P("lat", "lon"),
            P(),
        ),
        out_specs=(
            P("lat", "lon", None),
            P("lat", "lon", None),
            P(("lat", "lon"), None, None, None),
        ),
        check_vma=False,
    )
```
